256 devices in a mesh: dp: 64 (over z, y, x_lo), mp: 4 (over x_hi, core).
Axes of the slice: x: 4 (x_hi: 2, x_lo: 2; x = x_hi * 2 + x_lo), y: 4, z: 8, core: 2. Of those that a mesh axis runs over, the one named last changes fastest.
Arguments:
- inputs: bfloat16 [128, 256, 1152], P('dp', 'mp'), may hold values from -6 to 6
- cotangent: bfloat16 [128, 256, 1152], P('dp', 'mp'), may hold values from -16 to 16
- lengths: int32 [128], P('dp'), may hold values from 64 to 256
- up_weight: bfloat16 [1152, 6144], P(None, 'mp'), may hold values from -0.1875 to 0.1875
- down_weight: bfloat16 [6144, 1152], P('mp'), may hold values from -0.1875 to 0.1875
- clip_ratio: float32 [1], replicated, may hold values from 0.8 to 1.3
- count_noise: float32 [1], replicated, may hold values from -40 to 40
Outputs:
- grad_down: float32 [6144, 1152], P(('mp', 'dp'))
- ratio_next: float32 [1], replicated
The draws below stay inside these ranges and needn't reach their ends.
All inputs are finite; a program needn't handle non-finite values.
Results may differ from the reference program's by a relative error of at most 0.0029.
Values may be sent and summed in bfloat16 or wider, within the bound.
No kernel may reach another device: no remote copies, remote signals or barrier semaphores. Data moves between devices by JAX's collectives and lax.ppermute only.
A program may use at most 128 MiB of HBM per device.

```python
import math
import jax
import jax.numpy as jnp
from jax import lax

D = 1152
FF = 6144
SEQ = 256
EXAMPLES = 128


def draw_lengths(key, part):
    key = jax.random.fold_in(key, 7)
    values = jax.random.randint(key, (EXAMPLES,), SEQ // 4, SEQ + 1).astype(jnp.int32)
    values = values.at[0].set(SEQ)
    values = values.at[1].set(SEQ // 4)
    return values


def raised(array, rng, source, target, parts, factor):
    def block_of(axis_at):
        return (jnp.arange(array.shape[axis_at]) // (array.shape[axis_at] // parts)).reshape((-1,) + (1,) * (array.ndim - 1 - axis_at))

    near = jax.random.permutation(rng, parts)[block_of(target)]
    other_side = (block_of(target) + parts // 2) % parts
    return jnp.where((block_of(source) == near) | (block_of(source) == other_side), factor * array, array)


def level_of(own_key, shape, cuts, least, top_value):
    factor_of, own = 1.0, jax.random.fold_in(own_key, 6)
    for dim, shards_of in cuts:
        steps = jnp.exp(jax.random.uniform(jax.random.fold_in(own, dim), (shards_of,), jnp.float32, least / len(cuts), top_value / len(cuts)))
        factor_of = factor_of * jnp.repeat(steps, shape[dim] // shards_of).reshape([-1 if axis == dim else 1 for axis in range(len(shape))])
    return factor_of


def noise(rng, dims, scale, reach, shards=(), kind=jnp.bfloat16):
    array = jax.random.normal(rng, dims, jnp.float32) * scale
    if len(shards) > 0:
        array = level_of(rng, dims, shards, -0.22, 0.18) * array
    return jnp.clip(array, min=-reach, max=reach).astype(kind)


def gaussian_with(stream_key, shape, spread, bound, cuts, heavy, held_as=jnp.bfloat16):
    drawn = spread * jax.random.normal(stream_key, shape, jnp.float32)
    if cuts:
        drawn = drawn * level_of(stream_key, shape, cuts, -0.22, 0.18)
    return jnp.clip(raised(drawn, jax.random.fold_in(stream_key, 3), *heavy), -bound, bound).astype(held_as)


def setup_inputs(seed: int = 0) -> dict:
    streams_of = jax.random.split(jax.random.key(seed), 8)
    return {
        "inputs": noise(streams_of[0], (EXAMPLES, SEQ, D), 1.0, 6.0, ((0, 64), (1, 4))),
        "cotangent": gaussian_with(streams_of[1], (EXAMPLES, SEQ, D), 1.0, 16.0, ((0, 64), (1, 4)), (0, 2, 64, 4.0)),
        "lengths": draw_lengths(jax.random.fold_in(streams_of[7], 71), 0),
        "up_weight": noise(streams_of[3], (D, FF), D ** -0.5, 0.1875, ((1, 4),)),
        "down_weight": noise(streams_of[4], (FF, D), D ** -0.5, 0.1875, ((0, 4),)),
        "clip_ratio": jnp.clip(jnp.exp(jax.random.uniform(streams_of[5], (1,), jnp.float32, math.log(0.8), math.log(1.3))), 0.8, 1.3),
        "count_noise": noise(streams_of[6], (1,), (EXAMPLES / 20), 40.0, (), jnp.float32),
    }


curve_scale = 0.7978845608028654
cubic_term = 0.044715
target_share = 0.5

def gelu_parts(preact):
    cubic = preact * preact * preact
    tangent = jnp.tanh(curve_scale * (preact + cubic_term * cubic))
    values = 0.5 * preact * (1.0 + tangent)
    slopes = 0.5 * (1.0 + tangent) + 0.5 * preact * (1.0 - tangent * tangent) * curve_scale * (1.0 + 3.0 * cubic_term * preact * preact)
    return (values, slopes)

def example_pass(inputs_row, cotan_row, up_weight, down_weight):
    preact = jnp.dot(inputs_row, up_weight, preferred_element_type=jnp.float32)
    values, slopes = gelu_parts(preact)
    hidden = values.astype(jnp.bfloat16)
    backward = lax.dot_general(cotan_row, down_weight, (((1,), (1,)), ((), ())), preferred_element_type=jnp.float32)
    delta = (backward * slopes).astype(jnp.bfloat16)
    return (hidden, delta)

def gram(matrix):
    return lax.dot_general(matrix, matrix, (((1,), (1,)), ((), ())), preferred_element_type=jnp.float32)

def outer_sum(left, right):
    return lax.dot_general(left, right, (((0,), (0,)), ((), ())), preferred_element_type=jnp.float32)

def reference(inputs, cotangent, lengths, up_weight, down_weight, clip_ratio, count_noise):
    positions = jnp.arange(SEQ, dtype=jnp.int32)
    keep = (positions[None, :] < lengths[:, None]).astype(jnp.bfloat16)
    masked = cotangent * keep[:, :, None]

    def norm_of(pair):
        inputs_row, cotan_row = pair
        hidden, delta = example_pass(inputs_row, cotan_row, up_weight, down_weight)
        first = jnp.sum(gram(inputs_row) * gram(delta))
        second = jnp.sum(gram(hidden) * gram(cotan_row))
        return first + second
    squares = lax.map(norm_of, (inputs, masked))
    norms = jnp.sqrt(squares)
    clip = clip_ratio[0] * jnp.sqrt(jnp.float32(SEQ * D * FF))
    factors = clip / jnp.maximum(norms, clip)

    def grad_step(carry, triple):
        inputs_row, cotan_row, factor = triple
        hidden, delta = example_pass(inputs_row, cotan_row, up_weight, down_weight)
        down_term = outer_sum(hidden, cotan_row)
        return (carry + factor * down_term, None)
    zeros = jnp.zeros((FF, D), jnp.float32)
    sums, _ = lax.scan(grad_step, zeros, (inputs, masked, factors))
    grad_down = sums / EXAMPLES
    soft = jax.nn.sigmoid(4.0 * (clip - norms) / clip)
    share = (jnp.sum(soft) + count_noise[0]) / EXAMPLES
    ratio_next = clip_ratio * jnp.exp(-(share - target_share))
    return (grad_down, ratio_next)
```

```python
import jax
import jax.numpy as jnp
import numpy as np
from jax import lax
from jax.sharding import PartitionSpec as P

D = 1152
FF = 6144
SEQ = 256
AXES = ("dp", "mp")

curve_scale = 0.7978845608028654
cubic_term = 0.044715
target_share = 0.5

X, Y, Z, CORES = 4, 4, 8, 2


def coords(i):
    dp, mp = divmod(i, 4)
    z, rest = divmod(dp, 8)
    y, x_lo = divmod(rest, 2)
    x_hi, core = divmod(mp, 2)
    return (x_hi * 2 + x_lo, y, z, core)


def index_of(x, y, z, core):
    x, y, z = x % X, y % Y, z % Z
    return (z * 8 + y * 2 + x % 2) * 4 + (x // 2) * 2 + core


def permute(array, move):
    pairs = [(i, index_of(*move(*coords(i)))) for i in range(X * Y * Z * CORES)]
    return lax.ppermute(array, AXES, pairs)


def z_even(z, y):
    return (z ^ 1, y)


def z_odd(z, y):
    return ((((z - 1) % Z) ^ 1) + 1) % Z, y


def y_even(z, y):
    return (z, y ^ 1)


def y_odd(z, y):
    return (z, ((((y - 1) % Y) ^ 1) + 1) % Y)


def z_far(z, y):
    return ((z + 4) % Z, y)


STEPS = (
    ((z_even, z_odd, y_even, y_odd, z_far), (z_odd, z_even, y_even, y_odd, z_far)),
    ((y_even, y_odd, z_even, z_odd, z_far), (y_odd, y_even, z_even, z_odd, z_far)),
)


def block_orders(steps):
    places = [(z, y) for z in range(Z) for y in range(Y)]
    orders = {place: [place] for place in places}
    for step in reversed(steps):
        orders = {place: orders[place] + orders[step(*place)] for place in places}
    return orders


def row_table():
    table = np.zeros((CORES, Z, Y, 2, Z * Y), np.int32)
    for core in range(CORES):
        for chain in range(2):
            for (z, y), order in block_orders(STEPS[core][chain]).items():
                assert len(set(order)) == Z * Y
                table[core, z, y, chain] = [zb * Y + yb for zb, yb in order]
    return table


def exchange(array, number, chain):
    def move(x, y, z, core):
        z, y = STEPS[core][chain][number](z, y)
        return (x, y, z, core)

    return permute(array, move)


def gelu_parts(preact):
    cubic = preact * preact * preact
    tangent = jnp.tanh(curve_scale * (preact + cubic_term * cubic))
    values = 0.5 * preact * (1.0 + tangent)
    slopes = 0.5 * (1.0 + tangent) + 0.5 * preact * (1.0 - tangent * tangent) * curve_scale * (
        1.0 + 3.0 * cubic_term * preact * preact
    )
    return (values, slopes)


def batch_gram(matrix):
    return jnp.einsum("bsd,btd->bst", matrix, matrix, preferred_element_type=jnp.float32)


def right(x, y, z, core):
    return (x + 1, y, z, core)


def left(x, y, z, core):
    return (x - 1, y, z, core)


def other_core(x, y, z, core):
    return (x, y, z, 1 - core)


def swap_cores(*arrays):
    sent = jnp.concatenate(arrays, axis=0)
    got = permute(sent, other_core)
    return jnp.split(got, len(arrays), axis=0)


def example_pass(inputs, masked, up, down):
    preact = jnp.einsum("bsd,df->bsf", inputs, up, preferred_element_type=jnp.float32)
    values, slopes = gelu_parts(preact)
    hidden = values.astype(jnp.bfloat16)
    backward = jnp.einsum("bsd,fd->bsf", masked, down, preferred_element_type=jnp.float32)
    delta = (backward * slopes).astype(jnp.bfloat16)
    first = jnp.sum(batch_gram(inputs) * batch_gram(delta), axis=(1, 2))
    second = jnp.sum(batch_gram(hidden) * batch_gram(masked), axis=(1, 2))
    return hidden, first + second


def per_device(inputs, cotangent, lengths, up_weight, down_weight, clip_ratio, count_noise):
    dp = lax.axis_index("dp")
    mp = lax.axis_index("mp")
    z, y, x_lo, core = dp // 8, (dp // 2) % 4, dp % 2, mp % 2
    local = inputs.shape[1]

    positions = mp * local + lax.broadcasted_iota(jnp.int32, (lengths.shape[0], local), 1)
    keep = (positions < lengths[:, None]).astype(jnp.bfloat16)
    masked = cotangent * keep[:, :, None]

    in_l = permute(inputs, right)
    co_r = permute(masked, left)
    co_l = permute(masked, right)
    in_r = permute(inputs, left)
    in_o = permute(in_l, right)
    co_o = permute(co_r, left)
    in_s, co_s = swap_cores(inputs, masked)
    in_ls, co_rs = swap_cores(in_l, co_r)
    co_ls, in_rs = swap_cores(co_l, in_r)
    in_os, co_os = swap_cores(in_o, co_o)

    table = jnp.asarray(row_table())
    order = lax.dynamic_slice(table, (core, z, y, 0, 0), (1, 1, 1, 2, Z * Y)).reshape(2, 2, 16)
    order = jnp.stack([order[:, 1], order[:, 0]])
    rows = (
        order[..., None] * 48
        + x_lo * 24
        + jnp.arange(2, dtype=jnp.int32)[None, :, None, None] * 12
        + jnp.arange(12, dtype=jnp.int32)
    ).reshape(-1)
    units = up_weight.shape[1]
    pick = (lax.broadcasted_iota(jnp.int32, (units, rows.shape[0]), 0) == rows[None, :]).astype(jnp.bfloat16)
    up = jnp.einsum("df,fp->dp", up_weight, pick, preferred_element_type=jnp.bfloat16)
    down = jnp.einsum("fp,fd->pd", pick, down_weight, preferred_element_type=jnp.bfloat16)

    in_theirs = jnp.concatenate([in_l, in_ls, in_r, in_rs], axis=1)
    co_theirs = jnp.concatenate([co_l, co_ls, co_r, co_rs], axis=1)
    in_ours = jnp.concatenate([inputs, in_s, in_o, in_os], axis=1)
    co_ours = jnp.concatenate([masked, co_s, co_o, co_os], axis=1)
    hidden_theirs, squares_theirs = example_pass(in_theirs, co_theirs, up, down)
    hidden_ours, squares_ours = example_pass(in_ours, co_ours, up, down)

    both = jnp.stack([squares_ours, squares_theirs])
    both = jnp.where(x_lo == 0, both, both[::-1])
    for move in (other_core, lambda x, y, z, core: (x ^ 1, y, z, core), lambda x, y, z, core: (x ^ 2, y, z, core)):
        both = both + permute(both, move)
    norms_both = jnp.sqrt(both)
    clip = clip_ratio[0] * jnp.sqrt(jnp.float32(SEQ * D * FF))
    factors = clip / jnp.maximum(norms_both, clip)
    factors = jnp.where(x_lo == 0, factors, factors[::-1])
    norms = jnp.where(x_lo == 0, norms_both[0], norms_both[1])
    examples_all = lax.axis_size("dp") * lengths.shape[0]
    soft = jax.nn.sigmoid(4.0 * (clip - norms) / clip)
    count_total = jnp.sum(lax.all_gather(soft, "dp", axis=0, tiled=True))
    share = (count_total + count_noise[0]) / examples_all
    ratio_next = clip_ratio * jnp.exp(-(share - target_share))

    scale = (factors / examples_all).reshape(-1)

    def outer(lo, hi):
        hidden = jnp.concatenate([hidden_ours[:, :, lo:hi], hidden_theirs[:, :, lo:hi]], axis=0)
        cotan = jnp.concatenate([co_ours, co_theirs], axis=0)
        pieces = jnp.einsum("bsf,bsd->bfd", hidden, cotan, preferred_element_type=jnp.float32)
        return jnp.sum(scale[:, None, None] * pieces, axis=0)

    half = rows.shape[0] // 2
    quarter = half // 2
    sends = outer(0, half).astype(jnp.bfloat16)
    keeps = outer(half, 2 * half)
    got = [exchange(sends[chain * quarter : (chain + 1) * quarter], 0, chain) for chain in range(2)]
    sums = [keeps[chain * quarter : (chain + 1) * quarter] + got[chain].astype(jnp.float32) for chain in range(2)]
    size = quarter // 2
    got = [exchange(sums[chain][size:].astype(jnp.bfloat16), 1, chain) for chain in range(2)]
    sums = [sums[chain][:size] + got[chain].astype(jnp.float32) for chain in range(2)]
    total = jnp.stack(sums)
    for number in (2, 3, 4):
        size = size // 2
        got = exchange(total[:, size:].astype(jnp.bfloat16), number, 0)
        total = total[:, :size] + got.astype(jnp.float32)
    grad_down = total.reshape(-1, total.shape[-1])
    return (grad_down, ratio_next)


def solution(mesh):
    return jax.shard_map(
        per_device,
        mesh=mesh,
        in_specs=(
            P("dp", "mp", None),
            P("dp", "mp", None),
            P("dp"),
            P(None, "mp"),
            P("mp", None),
            P(),
            P(),
        ),
        out_specs=(P(("mp", "dp"), None), P()),
        check_vma=False,
    )
```

```python
import jax
import jax.numpy as jnp
import numpy as np
from jax import lax
from jax.experimental import pallas as pl
from jax.experimental.pallas import tpu as pltpu
from jax.sharding import PartitionSpec as P

D = 1152
FF = 6144
SEQ = 256
AXES = ("dp", "mp")

curve_scale = 0.7978845608028654
cubic_term = 0.044715
target_share = 0.5

X, Y, Z, CORES = 4, 4, 8, 2


def coords(i):
    dp, mp = divmod(i, 4)
    z, rest = divmod(dp, 8)
    y, x_lo = divmod(rest, 2)
    x_hi, core = divmod(mp, 2)
    return (x_hi * 2 + x_lo, y, z, core)


def index_of(x, y, z, core):
    x, y, z = x % X, y % Y, z % Z
    return (z * 8 + y * 2 + x % 2) * 4 + (x // 2) * 2 + core


def permute(array, move):
    pairs = [(i, index_of(*move(*coords(i)))) for i in range(X * Y * Z * CORES)]
    return lax.ppermute(array, AXES, pairs)


def z_even(z, y):
    return (z ^ 1, y)


def z_odd(z, y):
    return ((((z - 1) % Z) ^ 1) + 1) % Z, y


def y_even(z, y):
    return (z, y ^ 1)


def y_odd(z, y):
    return (z, ((((y - 1) % Y) ^ 1) + 1) % Y)


STEPS = (
    ((z_even, z_odd), (z_odd, z_even)),
    ((y_even, y_odd), (y_odd, y_even)),
)


def group_of(core, z, y):
    if core == 0:
        return [(zb, yb) for zb in sorted((z, (z + 4) % Z)) for yb in range(Y)]
    return [(zb, y) for zb in range(Z)]


GROUPS = []
for _i in range(X * Y * Z * CORES):
    _x, _y, _z, _core = coords(_i)
    _group = [index_of(_x, yb, zb, _core) for zb, yb in group_of(_core, _z, _y)]
    if _group not in GROUPS:
        GROUPS.append(_group)


def row_table():
    table = np.zeros((CORES, Z, Y, 2, 2, 192), np.int32)
    for core in range(CORES):
        for chain in range(2):
            places = [(z, y) for z in range(Z) for y in range(Y)]
            orders = {place: group_of(core, *place) for place in places}
            for step in reversed(STEPS[core][chain]):
                orders = {place: orders[place] + orders[step(*place)] for place in places}
            for (z, y), order in orders.items():
                assert len(set(order)) == Z * Y
                rows = []
                for number, (zb, yb) in enumerate(order):
                    first = (16, 8)[number % 2]
                    cut = range(first) if chain == 0 else range(first, 24)
                    rows += [(zb * Y + yb) * 48 + row for row in cut]
                table[core, z, y, 0, chain] = rows[192:]
                table[core, z, y, 1, chain] = rows[:192]
    return table


def exchange(array, number, chain):
    def move(x, y, z, core):
        z, y = STEPS[core][chain][number](z, y)
        return (x, y, z, core)

    return permute(array, move)


def gelu_parts(preact):
    square = preact * preact
    half = 0.5 * jnp.tanh(preact * (curve_scale + (curve_scale * cubic_term) * square)) + 0.5
    values = preact * half
    slopes = half + values * (1.0 - half) * (2.0 * curve_scale + (6.0 * curve_scale * cubic_term) * square)
    return (values, slopes)


def dot(left, right, contract):
    return lax.dot_general(left, right, ((contract[:1], contract[1:]), ((), ())), preferred_element_type=jnp.float32)


VMEM = pl.BlockSpec(memory_space=pltpu.VMEM)
HBM = pl.BlockSpec(memory_space=pltpu.HBM)
LANES = (8, 128)
LARGE = 60


def call(kernel, name, outs, args, specs=None, out_specs=None, scratch=(), limit=16):
    return pl.pallas_call(
        kernel,
        out_shape=outs,
        in_specs=specs or [VMEM] * len(args),
        out_specs=out_specs or jax.tree.map(lambda _: VMEM, outs),
        scratch_shapes=scratch,
        compiler_params=pltpu.CompilerParams(vmem_limit_bytes=limit * 2**20),
        cost_estimate=pl.CostEstimate(flops=0, bytes_accessed=0, transcendentals=0),
        name=name,
    )(*args)


def array(shape, kind):
    return jax.ShapeDtypeStruct(shape, kind)


def mask_kernel(left, cotangent, out):
    for e in range(out.shape[0]):
        positions = lax.broadcasted_iota(jnp.int32, out.shape[1:], 0)
        value = cotangent[e].astype(jnp.float32)
        out[e] = jnp.where(positions < left[e, :1, :1], value, 0.0).astype(out.dtype)


def products_of(rows, masked, up, down):
    values, slopes = gelu_parts(dot(rows, up[...], (1, 0)))
    delta = dot(masked, down[...], (1, 0)) * slopes
    return values.astype(jnp.bfloat16), delta.astype(jnp.bfloat16)


def stacked(refs, e):
    return jnp.concatenate([ref[e] for ref in refs], axis=0)


def both_examples(refs):
    return jnp.concatenate([stacked(refs, e) for e in range(2)], axis=0)


def copy_of(source, target, sems, number):
    return pltpu.make_async_copy(source, target, sems.at[number])


def write_example(e, masked, hidden, outs, held, sems):
    hidden_held, masked_held = held
    hidden_held[e] = hidden.T
    masked_held[e] = masked
    copies = [copy_of(kept.at[e], out.at[e], sems, 2 * e + k) for k, (kept, out) in enumerate(zip(held, outs))]
    for copy in copies:
        copy.start()
    return copies


def load_all(sources, targets, sems):
    loads = [copy_of(source, target, sems, k) for k, (source, target) in enumerate(zip(sources, targets))]
    for load in loads:
        load.start()
    return loads


def wait_all(copies):
    for copy in copies:
        copy.wait()


def theirs_kernel(*refs):
    sources, refs = refs[:14], refs[14:]
    hidden_out, masked_out, squares_out, hidden_early, delta_early, *refs = refs
    hidden_held, delta_held, *refs = refs
    held, sems, load_sems, refs = refs[:2], refs[2], refs[3], refs[4:]
    loads = load_all(sources, refs, load_sems)
    wait_all(loads[:3])
    up, down = refs[2], refs[5]
    values, slopes = gelu_parts(dot(both_examples(refs[:2]), up[...], (1, 0)))
    hidden_held[...] = values.astype(jnp.bfloat16)
    wait_all(loads[3:6])
    delta_held[...] = (dot(both_examples(refs[3:5]), down[...], (1, 0)) * slopes).astype(jnp.bfloat16)
    copies = [copy_of(hidden_held, hidden_early, sems, 4), copy_of(delta_held, delta_early, sems, 5)]
    for copy in copies:
        copy.start()
    wait_all(loads[6:])
    inputs, cotans = refs[6:10], refs[10:14]
    for e in range(2):
        rows, masked = stacked(inputs, e), stacked(cotans, e)
        hidden, delta = products_of(rows, masked, up, down)
        copies += write_example(e, masked, hidden, (hidden_out, masked_out), held, sems)
        first = dot(rows, rows, (1, 1)) * dot(delta, delta, (1, 1))
        second = dot(hidden, hidden, (1, 1)) * dot(masked, masked, (1, 1))
        squares_out[e] = jnp.broadcast_to(jnp.sum(first + second), LANES)
    wait_all(copies)


def pass_outs(units, tokens, width):
    return (
        array((2, units, tokens), jnp.bfloat16),
        array((2, tokens, width), jnp.bfloat16),
        array((2, *LANES), jnp.float32),
    )


def pass_scratch(units, tokens, width):
    return [
        pltpu.VMEM((2, units, tokens), jnp.bfloat16),
        pltpu.VMEM((2, tokens, width), jnp.bfloat16),
        pltpu.SemaphoreType.DMA((6,)),
    ]


def load_scratch(args):
    return [pltpu.SemaphoreType.DMA((len(args),))] + [pltpu.VMEM(arg.shape, arg.dtype) for arg in args]


def theirs_pass(inputs, cotans, own, up, down):
    width, units = up.shape
    tokens = 4 * inputs[0].shape[1]
    early = array((tokens, units), jnp.bfloat16)
    args = (*own[:2], up, *own[2:], down, *inputs, *cotans)
    return call(
        theirs_kernel,
        "theirs_pass",
        pass_outs(units, tokens, width) + (early, early),
        args,
        specs=[HBM] * 14,
        out_specs=(HBM, HBM, VMEM, HBM, HBM),
        scratch=[pltpu.VMEM(early.shape, early.dtype)] * 2 + pass_scratch(units, tokens, width) + load_scratch(args),
        limit=LARGE,
    )


def ours_kernel(*refs):
    sources, (hidden_out, masked_out, squares_out), refs = refs[:12], refs[12:15], refs[15:]
    held, sems, load_sems, refs = refs[:2], refs[2], refs[3], refs[4:]
    loads = load_all(sources, refs, load_sems)
    wait_all(loads[:3])
    up, down, hidden_early, delta_early = refs[2], refs[5], refs[10], refs[11]
    values, slopes = gelu_parts(dot(both_examples(refs[:2]), up[...], (1, 0)))
    hidden_late = values.astype(jnp.bfloat16)
    wait_all(loads[3:6])
    delta_late = (dot(both_examples(refs[3:5]), down[...], (1, 0)) * slopes).astype(jnp.bfloat16)
    wait_all(loads[6:])
    inputs, cotans = (*refs[6:8], *refs[:2]), (*refs[8:10], *refs[3:5])
    half = hidden_late.shape[0] // 2
    copies = []
    for e in range(2):
        at = slice(e * half, (e + 1) * half)
        rows, masked = stacked(inputs, e), stacked(cotans, e)
        hidden = jnp.concatenate([hidden_early[at, :], hidden_late[at, :]], axis=0)
        delta = jnp.concatenate([delta_early[at, :], delta_late[at, :]], axis=0)
        copies += write_example(e, masked, hidden, (hidden_out, masked_out), held, sems)
        first = dot(rows, rows, (1, 1)) * dot(delta, delta, (1, 1))
        second = dot(hidden, hidden, (1, 1)) * dot(masked, masked, (1, 1))
        squares_out[e] = jnp.broadcast_to(jnp.sum(first + second), LANES)
    wait_all(copies)


def ours_pass(early, up, down, inputs, cotans):
    width, units = up.shape
    tokens = 4 * inputs[0].shape[1]
    args = (*inputs[2:], up, *cotans[2:], down, *inputs[:2], *cotans[:2], *early)
    return call(
        ours_kernel,
        "ours_pass",
        pass_outs(units, tokens, width),
        args,
        specs=[HBM] * len(args),
        out_specs=(HBM, HBM, VMEM),
        scratch=pass_scratch(units, tokens, width) + load_scratch(args),
        limit=LARGE,
    )


def factors_kernel(examples, first, clip, chip, across, from_left, from_right, scale, count):
    total = (chip[...] + across[...]) + (from_left[...] + from_right[...])
    norms = jnp.sqrt(total)
    threshold = clip[...]
    factors = threshold / jnp.maximum(norms, threshold)
    swapped = jnp.concatenate([factors[2:], factors[:2]], axis=0)
    scale[...] = jnp.where(first[...] == 1, factors, swapped) * (1.0 / examples)
    soft = jnp.floor(jax.nn.sigmoid(4.0 * (threshold - norms) / threshold) * 131072.0 + 0.5) * (1.0 / 131072.0)
    count[...] = (soft[0] + soft[1]) + (soft[2] + soft[3])


TAIL = 16


def tail_rows(count, rows, width):
    count = count[:1, :1]
    whole = jnp.floor(count)
    rest = count - whole
    second = jnp.floor(rest * 256.0) * (1.0 / 256.0)
    rest = rest - second
    third = jnp.floor(rest * 65536.0) * (1.0 / 65536.0)
    row = lax.broadcasted_iota(jnp.int32, (8, 128), 0)
    parts = jnp.where(row == 0, whole, jnp.where(row == 1, second, jnp.where(row == 2, third, rest - third)))
    parts = jnp.where(row < 4, parts, 0.0)
    if width > 128:
        parts = jnp.concatenate([parts, jnp.zeros((8, width - 128), jnp.float32)], axis=1)
    return parts, jnp.zeros((rows - 8, width), jnp.float32)


def count_in(tail):
    return jnp.broadcast_to(jnp.sum(tail[:8, :128], axis=0, keepdims=True), LANES)


def outer_rows(scale, hidden, masked, loads):
    total = None
    for e in range(4):
        wait_all(loads[2 * e : 2 * e + 2])
        piece = scale[e, :1, :1] * dot(hidden[e], masked[e], (1, 0))
        total = piece if total is None else total + piece
    return total


def load_outer(first, refs, hidden, masked, sems):
    rows = hidden.shape[1]
    loads = []
    for e in range(4):
        hidden_from, masked_from = refs[e // 2], refs[2 + e // 2]
        loads.append(copy_of(hidden_from.at[e % 2, pl.ds(first, rows)], hidden.at[e], sems, 2 * e))
        loads.append(copy_of(masked_from.at[e % 2], masked.at[e], sems, 2 * e + 1))
    for load in loads:
        load.start()
    return loads


def outer_send_kernel(scale, count, *refs):
    operands, (out0, out1), (hidden, masked, sems) = refs[:4], refs[4:6], refs[6:]
    rows, width = out1.shape
    total = outer_rows(scale, hidden, masked, load_outer(0, operands, hidden, masked, sems))
    out0[...] = jnp.concatenate([total[:rows], *tail_rows(count[...], TAIL, width)], axis=0).astype(out0.dtype)
    out1[...] = total[rows:].astype(out1.dtype)


def outer_keep_kernel(scale, *refs):
    operands, outs, (hidden, masked, sems) = refs[:4], refs[4:6], refs[6:]
    rows = outs[0].shape[0]
    total = outer_rows(scale, hidden, masked, load_outer(2 * rows, operands, hidden, masked, sems))
    outs[0][...] = total[:rows]
    outs[1][...] = total[rows:]


def outer(kernel, name, rows, tail, kind, scalars, operands):
    _, tokens, width = operands[2].shape
    return call(
        kernel,
        name,
        (array((rows + tail, width), kind), array((rows, width), kind)),
        (*scalars, *operands),
        specs=[VMEM] * len(scalars) + [HBM] * 4,
        scratch=[
            pltpu.VMEM((4, 2 * rows, tokens), jnp.bfloat16),
            pltpu.VMEM((4, tokens, width), jnp.bfloat16),
            pltpu.SemaphoreType.DMA((8,)),
        ],
        limit=LARGE,
    )


def step_first_kernel(count, kept, got, count_out, keep, send):
    rows, width = kept.shape
    half = rows // 2
    message = got[...].astype(jnp.float32)
    total = kept[...] + message[:rows]
    keep[...] = total[:half]
    counted = count[...] + count_in(message[rows:])
    count_out[...] = counted
    send[...] = jnp.concatenate([total[half:], *tail_rows(counted, TAIL, width)], axis=0).astype(send.dtype)


def step_outs(kept, sent, width):
    return (array(LANES, jnp.float32), array((kept, width), jnp.float32), array((sent, width), jnp.bfloat16))


def step_first(count, kept, got):
    rows, width = kept.shape
    return call(step_first_kernel, "step_first", step_outs(rows // 2, rows // 2 + TAIL, width), (count, kept, got))


def step_second_kernel(kept, got, keep, send):
    half = kept.shape[0] // 2
    total = kept[...] + got[...].astype(jnp.float32)
    keep[...] = total[:half]
    send[...] = total[half:].astype(send.dtype)


def step_second(kept, got):
    rows, width = kept.shape
    outs = (array((rows // 2, width), jnp.float32), array((rows // 2, width), jnp.bfloat16))
    return call(step_second_kernel, "step_second", outs, (kept, got))


SIDE = 128


def step_join_kernel(count, kept0, kept1, got0, got1, send):
    rows, width = kept0.shape
    message = got0[...].astype(jnp.float32)
    total0 = kept0[...] + message[:rows]
    total1 = kept1[...] + got1[...].astype(jnp.float32)
    counted = count[...] + count_in(message[rows:])
    pieces = []
    for at in range(0, rows, 24):
        pieces += [total0[at : at + 16], total1[at : at + 8], total0[at + 16 : at + 24], total1[at + 8 : at + 24]]
    side = tail_rows(counted, 24, SIDE)
    side = jnp.concatenate(list(side) * (rows // 12), axis=0)
    send[...] = jnp.concatenate([jnp.concatenate(pieces, axis=0), side], axis=1).astype(send.dtype)


def step_join(count, kept0, kept1, got0, got1):
    rows, width = kept0.shape
    return call(step_join_kernel, "step_join", array((2 * rows, width + SIDE), jnp.bfloat16), (count, kept0, kept1, got0, got1))


def step_last_kernel(got, out, count):
    rows, width = out.shape
    message = got[...].astype(jnp.float32)
    chunks = [message[at : at + rows] for at in range(0, message.shape[0], rows)]
    while len(chunks) > 1:
        chunks = [a + b for a, b in zip(chunks[::2], chunks[1::2])]
    out[...] = chunks[0][:, :width]
    count[...] = jnp.broadcast_to(jnp.sum(chunks[0][:8, width:], axis=0, keepdims=True), LANES)


def step_last(got, rows, width):
    outs = (array((rows, width), jnp.float32), array(LANES, jnp.float32))
    return call(step_last_kernel, "step_last", outs, (got,))


def right(x, y, z, core):
    return (x + 1, y, z, core)


def left(x, y, z, core):
    return (x - 1, y, z, core)


def other_core(x, y, z, core):
    return (x, y, z, 1 - core)


def opposite(x, y, z, core):
    return (x + 2, y, z, core)


def swap_cores(*arrays):
    return [permute(array, other_core) for array in arrays]


def after(array, *others):
    return lax.optimization_barrier((array, *others))[0]


def per_device(inputs, cotangent, lengths, up_weight, down_weight, clip_ratio, count_noise):
    dp = lax.axis_index("dp")
    mp = lax.axis_index("mp")
    z, y, x_lo, core = dp // 8, (dp // 2) % 4, dp % 2, mp % 2
    local = inputs.shape[1]

    units = up_weight.shape[1]

    in_l = permute(inputs, right)
    in_r = permute(inputs, left)
    real = jnp.broadcast_to((lengths - mp * local)[:, None, None], (lengths.shape[0], *LANES))
    masked = call(mask_kernel, "mask", array(cotangent.shape, cotangent.dtype), (real, cotangent))
    co_r = permute(masked, left)
    co_l = permute(masked, right)
    in_s, co_s = swap_cores(inputs, masked)

    table = jnp.asarray(row_table())
    rows = lax.dynamic_slice(table, (core, z, y, 0, 0, 0), (1, 1, 1, 2, 2, 192)).reshape(-1) + x_lo * 24
    pick = (lax.broadcasted_iota(jnp.int32, (units, rows.shape[0]), 0) == rows[None, :]).astype(jnp.bfloat16)
    up = jnp.einsum("df,fp->dp", up_weight, pick, preferred_element_type=jnp.bfloat16)
    down = jnp.einsum("fd,fp->dp", down_weight, pick, preferred_element_type=jnp.bfloat16)

    in_o = permute(after(in_l, up, down), right)
    co_o = permute(after(co_r, up, down), left)
    in_ls, in_rs, co_ls, co_rs = swap_cores(in_l, in_r, co_l, co_r)
    hidden_theirs, masked_theirs, squares_theirs, *early = theirs_pass(
        (in_l, in_ls, in_r, in_rs), (co_l, co_ls, co_r, co_rs), (inputs, in_s, masked, co_s), up, down
    )
    in_os, co_os = swap_cores(after(in_o, squares_theirs), after(co_o, squares_theirs))
    hidden_ours, masked_ours, squares_ours = ours_pass(early, up, down, (inputs, in_s, in_o, in_os), (masked, co_s, co_o, co_os))

    first = jnp.where(x_lo == 0, squares_ours, squares_theirs)
    second = jnp.where(x_lo == 0, squares_theirs, squares_ours)
    both = jnp.concatenate([first, second], axis=0)
    both = both + permute(both, other_core)
    examples_all = lax.axis_size("dp") * lengths.shape[0]
    clip = clip_ratio[0] * jnp.sqrt(jnp.float32(SEQ * D * FF))
    scale, count = call(
        lambda *refs: factors_kernel(examples_all, *refs),
        "factors",
        (array((4, *LANES), jnp.float32), array(LANES, jnp.float32)),
        (
            jnp.broadcast_to((x_lo == 0).astype(jnp.int32), LANES),
            jnp.broadcast_to(clip, LANES),
            both,
            permute(both, opposite),
            permute(both, right),
            permute(both, left),
        ),
    )

    quarter = rows.shape[0] // 4
    operands = (hidden_ours, hidden_theirs, masked_ours, masked_theirs)
    send0, send1 = outer(outer_send_kernel, "outer_send", quarter, TAIL, jnp.bfloat16, (scale, count), operands)
    got0, got1 = exchange(send0, 0, 0), exchange(send1, 0, 1)
    keep0, keep1 = outer(outer_keep_kernel, "outer_keep", quarter, 0, jnp.float32, (scale,), operands)
    count, keep0, send0 = step_first(count, keep0, got0)
    got0 = exchange(send0, 1, 0)
    keep1, send1 = step_second(keep1, got1)
    got1 = exchange(send1, 1, 1)
    send = step_join(count, keep0, keep1, got0, got1)
    got = lax.all_to_all(send, AXES, 0, 0, axis_index_groups=GROUPS, tiled=True)
    grad_down, count = step_last(got, 4 * quarter // (Z * Y), send.shape[1] - SIDE)
    share = (count[0, 0] + count_noise[0]) / examples_all
    ratio_next = clip_ratio * jnp.exp(-(share - target_share))
    return (grad_down, ratio_next)


def solution(mesh):
    return jax.shard_map(
        per_device,
        mesh=mesh,
        in_specs=(
            P("dp", "mp", None),
            P("dp", "mp", None),
            P("dp"),
            P(None, "mp"),
            P("mp", None),
            P(),
            P(),
        ),
        out_specs=(P(("mp", "dp"), None), P()),
        check_vma=False,
    )
```

```python
import jax
import jax.numpy as jnp
import numpy as np
from jax import lax
from jax.experimental import pallas as pl
from jax.experimental.pallas import tpu as pltpu
from jax.sharding import PartitionSpec as P

D = 1152
FF = 6144
SEQ = 256
AXES = ("dp", "mp")

curve_scale = 0.7978845608028654
cubic_term = 0.044715
target_share = 0.5

X, Y, Z, CORES = 4, 4, 8, 2


def coords(i):
    dp, mp = divmod(i, 4)
    z, rest = divmod(dp, 8)
    y, x_lo = divmod(rest, 2)
    x_hi, core = divmod(mp, 2)
    return (x_hi * 2 + x_lo, y, z, core)


def index_of(x, y, z, core):
    x, y, z = x % X, y % Y, z % Z
    return (z * 8 + y * 2 + x % 2) * 4 + (x // 2) * 2 + core


def permute(array, move):
    pairs = [(i, index_of(*move(*coords(i)))) for i in range(X * Y * Z * CORES)]
    return lax.ppermute(array, AXES, pairs)


def z_even(z, y):
    return (z ^ 1, y)


def z_odd(z, y):
    return ((((z - 1) % Z) ^ 1) + 1) % Z, y


def y_even(z, y):
    return (z, y ^ 1)


def y_odd(z, y):
    return (z, ((((y - 1) % Y) ^ 1) + 1) % Y)


STEPS = (
    ((z_even, z_odd), (z_odd, z_even)),
    ((y_even, y_odd), (y_odd, y_even)),
)


def group_of(core, z, y):
    if core == 0:
        return [(zb, yb) for zb in sorted((z, (z + 4) % Z)) for yb in range(Y)]
    return [(zb, y) for zb in range(Z)]


GROUPS = []
for _i in range(X * Y * Z * CORES):
    _x, _y, _z, _core = coords(_i)
    _group = [index_of(_x, yb, zb, _core) for zb, yb in group_of(_core, _z, _y)]
    if _group not in GROUPS:
        GROUPS.append(_group)


def row_table():
    table = np.zeros((CORES, Z, Y, 2, 2, 192), np.int32)
    for core in range(CORES):
        for chain in range(2):
            places = [(z, y) for z in range(Z) for y in range(Y)]
            orders = {place: group_of(core, *place) for place in places}
            for step in reversed(STEPS[core][chain]):
                orders = {place: orders[place] + orders[step(*place)] for place in places}
            for (z, y), order in orders.items():
                assert len(set(order)) == Z * Y
                rows = []
                for number, (zb, yb) in enumerate(order):
                    first = (16, 8)[number % 2]
                    cut = range(first) if chain == 0 else range(first, 24)
                    rows += [(zb * Y + yb) * 48 + row for row in cut]
                table[core, z, y, 0, chain] = rows[192:]
                table[core, z, y, 1, chain] = rows[:192]
    return table.reshape(CORES * Z * Y, 1, -1)


def exchange(array, number, chain):
    def move(x, y, z, core):
        z, y = STEPS[core][chain][number](z, y)
        return (x, y, z, core)

    return permute(array, move)


def gelu_parts(preact):
    square = preact * preact
    half = 0.5 * jnp.tanh(preact * (curve_scale + (curve_scale * cubic_term) * square)) + 0.5
    values = preact * half
    slopes = half + values * (1.0 - half) * (2.0 * curve_scale + (6.0 * curve_scale * cubic_term) * square)
    return (values, slopes)


def dot(left, right, contract):
    return lax.dot_general(left, right, ((contract[:1], contract[1:]), ((), ())), preferred_element_type=jnp.float32)


VMEM = pl.BlockSpec(memory_space=pltpu.VMEM)
HBM = pl.BlockSpec(memory_space=pl.ANY)
LANES = (8, 128)


def call(kernel, name, outs, args, specs=None, scratch=(), flops=0, limit=12):
    return pl.pallas_call(
        kernel,
        out_shape=outs,
        in_specs=specs or [VMEM] * len(args),
        out_specs=jax.tree.map(lambda _: VMEM, outs),
        scratch_shapes=scratch,
        compiler_params=pltpu.CompilerParams(vmem_limit_bytes=limit * 2**20),
        cost_estimate=pl.CostEstimate(flops=flops, bytes_accessed=0, transcendentals=0),
        name=name,
    )(*args)


def array(shape, kind):
    return jax.ShapeDtypeStruct(shape, kind)


def place():
    dp, mp = lax.axis_index("dp"), lax.axis_index("mp")
    return dp // 8, (dp // 2) % 4, dp % 2, mp % 2


def mask_kernel(lengths, cotangent, out):
    positions = lax.axis_index("mp") * out.shape[1] + lax.broadcasted_iota(jnp.int32, out.shape[1:], 0)
    for e in range(out.shape[0]):
        value = cotangent[e].astype(jnp.float32)
        out[e] = jnp.where(positions < lengths[:, e : e + 1], value, 0.0).astype(out.dtype)


def load_rows(table, rows, sem):
    z, y, x_lo, core = place()
    copy = pltpu.make_async_copy(table.at[(core * Z + z) * Y + y], rows, sem)
    copy.start()
    copy.wait()
    return rows[...] + x_lo * 24


def up_kernel(table, weight, out, rows, sem):
    chosen = load_rows(table, rows, sem)
    pick = lax.broadcasted_iota(jnp.int32, (weight.shape[1], out.shape[1]), 0) == chosen
    out[...] = dot(weight[...], pick.astype(jnp.bfloat16), (1, 0)).astype(out.dtype)


def down_kernel(table, weight, out, rows, sem):
    chosen = load_rows(table, rows, sem).astype(jnp.float32)
    chosen = jnp.broadcast_to(chosen, (8, chosen.shape[1])).T[:, :1].astype(jnp.int32)
    pick = lax.broadcasted_iota(jnp.int32, (out.shape[0], weight.shape[0]), 1) == chosen
    out[...] = dot(pick.astype(jnp.bfloat16), weight[...], (1, 0)).astype(out.dtype)


def select(kernel, name, table, weight, shape, units):
    scratch = [pltpu.VMEM(table.shape[1:], jnp.int32), pltpu.SemaphoreType.DMA]
    return call(kernel, name, array(shape, weight.dtype), (table, weight), [HBM, VMEM], scratch, limit=16)


def products_of(rows, masked, up, down):
    values, slopes = gelu_parts(dot(rows, up[...], (1, 0)))
    delta = dot(masked, down[...], (1, 1)) * slopes
    return values.astype(jnp.bfloat16), delta.astype(jnp.bfloat16)


def stacked(refs, e):
    return jnp.concatenate([ref[e] for ref in refs], axis=0)


def both_examples(refs):
    return jnp.concatenate([stacked(refs, e) for e in range(2)], axis=0)


def square_of(rows, masked, hidden, delta):
    first = dot(rows, rows, (1, 1)) * dot(delta, delta, (1, 1))
    second = dot(hidden, hidden, (1, 1)) * dot(masked, masked, (1, 1))
    return jnp.broadcast_to(jnp.sum(first + second), LANES)


def early_kernel(in_a, in_b, co_a, co_b, up, down, hidden, delta):
    hidden[...], delta[...] = products_of(both_examples((in_a, in_b)), both_examples((co_a, co_b)), up, down)


def early_pass(inputs, cotans, up, down):
    out = array((4 * inputs[0].shape[1], up.shape[1]), jnp.bfloat16)
    return call(early_kernel, "early_pass", (out, out), (*inputs, *cotans, up, down))


def theirs_kernel(*refs):
    inputs, cotans = refs[:4], refs[4:8]
    up, down, hidden_out, masked_out, squares_out = refs[8:]
    for e in range(2):
        rows, masked = stacked(inputs, e), stacked(cotans, e)
        hidden, delta = products_of(rows, masked, up, down)
        hidden_out[e] = hidden.T
        masked_out[e] = masked
        squares_out[e] = square_of(rows, masked, hidden, delta)


def pass_outs(units, tokens, width, squares):
    return (
        array((2, units, tokens), jnp.bfloat16),
        array((2, tokens, width), jnp.bfloat16),
        array((squares, *LANES), jnp.float32),
    )


def theirs_pass(inputs, cotans, up, down):
    width, units = up.shape
    tokens = 4 * inputs[0].shape[1]
    return call(theirs_kernel, "theirs_pass", pass_outs(units, tokens, width, 2), (*inputs, *cotans, up, down))


def ours_kernel(*refs):
    inputs, cotans = refs[:4], refs[4:8]
    up, down, hidden_early, delta_early, theirs = refs[8:13]
    hidden_out, masked_out, squares_out = refs[13:]
    hidden_late, delta_late = products_of(both_examples(inputs[2:]), both_examples(cotans[2:]), up, down)
    half = hidden_late.shape[0] // 2
    is_first = place()[2] == 0
    for e in range(2):
        at = slice(e * half, (e + 1) * half)
        rows, masked = stacked(inputs, e), stacked(cotans, e)
        hidden = jnp.concatenate([hidden_early[at, :], hidden_late[at, :]], axis=0)
        delta = jnp.concatenate([delta_early[at, :], delta_late[at, :]], axis=0)
        hidden_out[e] = hidden.T
        masked_out[e] = masked
        square = square_of(rows, masked, hidden, delta)
        squares_out[e] = jnp.where(is_first, square, theirs[e])
        squares_out[2 + e] = jnp.where(is_first, theirs[e], square)


def ours_pass(inputs, cotans, up, down, early, theirs):
    width, units = up.shape
    tokens = 4 * inputs[0].shape[1]
    outs = pass_outs(units, tokens, width, 4)
    return call(ours_kernel, "ours_pass", outs, (*inputs, *cotans, up, down, *early, theirs))


def add_kernel(left, right, out):
    out[...] = left[...] + right[...]


def factors_of(examples, ratio, chip, across, from_left, from_right):
    total = (chip[...] + across[...]) + (from_left[...] + from_right[...])
    norms = jnp.sqrt(total)
    clip = ratio[...] * np.sqrt(np.float32(SEQ * D * FF))
    factors = clip / jnp.maximum(norms, clip)
    is_first = place()[2] == 0
    scale = jnp.where(is_first, factors, jnp.concatenate([factors[2:], factors[:2]], axis=0)) * (1.0 / examples)
    soft = jnp.floor(jax.nn.sigmoid(4.0 * (clip - norms) / clip) * 131072.0 + 0.5) * (1.0 / 131072.0)
    return scale, (soft[0] + soft[1]) + (soft[2] + soft[3])


TAIL = 16


def tail_rows(count, rows, width):
    count = count[:1, :1]
    whole = jnp.floor(count)
    rest = count - whole
    second = jnp.floor(rest * 256.0) * (1.0 / 256.0)
    rest = rest - second
    third = jnp.floor(rest * 65536.0) * (1.0 / 65536.0)
    row = lax.broadcasted_iota(jnp.int32, (8, 128), 0)
    parts = jnp.where(row == 0, whole, jnp.where(row == 1, second, jnp.where(row == 2, third, rest - third)))
    parts = jnp.where(row < 4, parts, 0.0)
    if width > 128:
        parts = jnp.concatenate([parts, jnp.zeros((8, width - 128), jnp.float32)], axis=1)
    return parts, jnp.zeros((rows - 8, width), jnp.float32)


def count_in(tail):
    return jnp.broadcast_to(jnp.sum(tail[:8, :128], axis=0, keepdims=True), LANES)


def outer_rows(at, rows, scale, operands):
    hidden_a, hidden_b, masked_a, masked_b = operands
    total = None
    for e in range(4):
        hidden, masked = ((hidden_a, masked_a), (hidden_b, masked_b))[e // 2]
        piece = scale[e, :1, :1] * dot(hidden[e % 2, at : at + rows, :], masked[e % 2], (1, 0))
        total = piece if total is None else total + piece
    return total


def outer_send_kernel(examples, *refs):
    small, operands, (out0, out1, count_out, scale_out) = refs[:5], refs[5:9], refs[9:]
    rows, width = out1.shape
    scale, count = factors_of(examples, *small)
    count_out[...] = count
    scale_out[...] = scale
    total = outer_rows(0, rows, scale, operands)
    out0[...] = jnp.concatenate([total, *tail_rows(count, TAIL, width)], axis=0).astype(out0.dtype)
    out1[...] = outer_rows(rows, rows, scale, operands).astype(out1.dtype)


def outer_keep_kernel(scale, *refs):
    operands, outs = refs[:4], refs[4:]
    rows = outs[0].shape[0]
    for chain, out in enumerate(outs):
        out[...] = outer_rows((2 + chain) * rows, rows, scale[...], operands)


def outer_send(rows, examples, small, operands):
    width = operands[2].shape[2]
    outs = (
        array((rows + TAIL, width), jnp.bfloat16),
        array((rows, width), jnp.bfloat16),
        array(LANES, jnp.float32),
        array((4, *LANES), jnp.float32),
    )
    return call(lambda *refs: outer_send_kernel(examples, *refs), "outer_send", outs, (*small, *operands))


def outer_keep(rows, scale, operands):
    outs = (array((rows, operands[2].shape[2]), jnp.float32),) * 2
    return call(outer_keep_kernel, "outer_keep", outs, (scale, *operands))


def step_first_kernel(count, kept, got, count_out, keep, send):
    rows, width = kept.shape
    half = rows // 2
    message = got[...].astype(jnp.float32)
    total = kept[...] + message[:rows]
    keep[...] = total[:half]
    counted = count[...] + count_in(message[rows:])
    count_out[...] = counted
    send[...] = jnp.concatenate([total[half:], *tail_rows(counted, TAIL, width)], axis=0).astype(send.dtype)


def step_outs(kept, sent, width):
    return (array(LANES, jnp.float32), array((kept, width), jnp.float32), array((sent, width), jnp.bfloat16))


def step_first(count, kept, got):
    rows, width = kept.shape
    return call(step_first_kernel, "step_first", step_outs(rows // 2, rows // 2 + TAIL, width), (count, kept, got))


def step_second_kernel(kept, got, keep, send):
    half = kept.shape[0] // 2
    total = kept[...] + got[...].astype(jnp.float32)
    keep[...] = total[:half]
    send[...] = total[half:].astype(send.dtype)


def step_second(kept, got):
    rows, width = kept.shape
    outs = (array((rows // 2, width), jnp.float32), array((rows // 2, width), jnp.bfloat16))
    return call(step_second_kernel, "step_second", outs, (kept, got))


SIDE = 128


def step_join_kernel(count, kept0, kept1, got0, got1, send):
    rows, width = kept0.shape
    message = got0[...].astype(jnp.float32)
    total0 = kept0[...] + message[:rows]
    total1 = kept1[...] + got1[...].astype(jnp.float32)
    counted = count[...] + count_in(message[rows:])
    pieces = []
    for at in range(0, rows, 24):
        pieces += [total0[at : at + 16], total1[at : at + 8], total0[at + 16 : at + 24], total1[at + 8 : at + 24]]
    side = tail_rows(counted, 24, SIDE)
    side = jnp.concatenate(list(side) * (rows // 12), axis=0)
    send[...] = jnp.concatenate([jnp.concatenate(pieces, axis=0), side], axis=1).astype(send.dtype)


def step_join(count, kept0, kept1, got0, got1):
    rows, width = kept0.shape
    return call(step_join_kernel, "step_join", array((2 * rows, width + SIDE), jnp.bfloat16), (count, kept0, kept1, got0, got1))


def step_last_kernel(examples, ratio, noise, got, out, ratio_next):
    rows, width = out.shape
    message = got[...].astype(jnp.float32)
    chunks = [message[at : at + rows] for at in range(0, message.shape[0], rows)]
    while len(chunks) > 1:
        chunks = [a + b for a, b in zip(chunks[::2], chunks[1::2])]
    out[...] = chunks[0][:, :width]
    count = jnp.sum(chunks[0][:8, width:], axis=0, keepdims=True)
    share = (count[:, :1] + noise[...]) / examples
    ratio_next[...] = ratio[...] * jnp.exp(-(share - target_share))


def step_last(examples, ratio, noise, got, rows, width):
    outs = (array((rows, width), jnp.float32), array((1, 1), jnp.float32))
    args = (ratio.reshape(1, 1), noise.reshape(1, 1), got)
    return call(lambda *refs: step_last_kernel(examples, *refs), "step_last", outs, args)


def right(x, y, z, core):
    return (x + 1, y, z, core)


def left(x, y, z, core):
    return (x - 1, y, z, core)


def other_core(x, y, z, core):
    return (x, y, z, 1 - core)


def opposite(x, y, z, core):
    return (x + 2, y, z, core)


def swap_cores(*arrays):
    return [permute(array, other_core) for array in arrays]


def after(array, *others):
    return lax.optimization_barrier((array, *others))[0]


def per_device(inputs, cotangent, lengths, up_weight, down_weight, clip_ratio, count_noise):
    in_l = permute(inputs, right)
    masked = call(
        mask_kernel, "mask", array(cotangent.shape, cotangent.dtype), (lengths.reshape(1, -1), cotangent)
    )
    co_r = permute(masked, left)

    table = jnp.asarray(row_table())
    width, units = up_weight.shape
    up = select(up_kernel, "select_up", table, up_weight, (width, units // 2), units // 2)
    down = select(down_kernel, "select_down", table, down_weight, (units // 2, width), units // 2)

    in_s, co_s = swap_cores(inputs, masked)
    co_l = permute(masked, right)
    in_r = permute(inputs, left)
    early = early_pass((inputs, in_s), (masked, co_s), up, down)
    ratio = permute(after(clip_ratio.reshape(1, 1), *early), other_core)
    in_l, co_r = after(in_l, ratio), after(co_r, ratio)
    in_o = permute(in_l, right)
    co_o = permute(co_r, left)
    in_ls, in_rs, co_ls, co_rs = swap_cores(in_l, in_r, co_l, co_r)
    in_os, co_os = swap_cores(in_o, co_o)
    hidden_theirs, masked_theirs, squares_theirs = theirs_pass((in_l, in_ls, in_r, in_rs), (co_l, co_ls, co_r, co_rs), up, down)
    hidden_ours, masked_ours, squares = ours_pass(
        (inputs, in_s, in_o, in_os), (masked, co_s, co_o, co_os), up, down, early, squares_theirs
    )

    chip = call(add_kernel, "chip_squares", array(squares.shape, squares.dtype), (squares, permute(squares, other_core)))
    small = (ratio, chip, *(permute(chip, move) for move in (opposite, right, left)))
    examples_all = lax.axis_size("dp") * lengths.shape[0]
    operands = (hidden_ours, hidden_theirs, masked_ours, masked_theirs)
    quarter = units // 8
    send0, send1, count, scale = outer_send(quarter, examples_all, small, operands)
    got0, got1 = exchange(send0, 0, 0), exchange(send1, 0, 1)
    keep0, keep1 = outer_keep(quarter, scale, operands)
    count, keep0, send0 = step_first(count, keep0, got0)
    got0 = exchange(send0, 1, 0)
    keep1, send1 = step_second(keep1, got1)
    got1 = exchange(send1, 1, 1)
    send = step_join(count, keep0, keep1, got0, got1)
    got = lax.all_to_all(send, AXES, 0, 0, axis_index_groups=GROUPS, tiled=True)
    grad_down, ratio_next = step_last(
        examples_all, ratio, count_noise, got, 4 * quarter // (Z * Y), send.shape[1] - SIDE
    )
    return (grad_down, ratio_next.reshape(1))


def solution(mesh):
    return jax.shard_map(
        per_device,
        mesh=mesh,
        in_specs=(
            P("dp", "mp", None),
            P("dp", "mp", None),
            P("dp"),
            P(None, "mp"),
            P("mp", None),
            P(),
            P(),
        ),
        out_specs=(P(("mp", "dp"), None), P()),
        check_vma=False,
    )
```

```python
import jax
import jax.numpy as jnp
import numpy as np
from jax import lax
from jax.experimental import pallas as pl
from jax.experimental.pallas import tpu as pltpu
from jax.sharding import PartitionSpec as P

D = 1152
FF = 6144
SEQ = 256
AXES = ("dp", "mp")

curve_scale = 0.7978845608028654
cubic_term = 0.044715
target_share = 0.5

X, Y, Z, CORES = 4, 4, 8, 2


def coords(i):
    dp, mp = divmod(i, 4)
    z, rest = divmod(dp, 8)
    y, x_lo = divmod(rest, 2)
    x_hi, core = divmod(mp, 2)
    return (x_hi * 2 + x_lo, y, z, core)


def index_of(x, y, z, core):
    x, y, z = x % X, y % Y, z % Z
    return (z * 8 + y * 2 + x % 2) * 4 + (x // 2) * 2 + core


def permute(array, move):
    pairs = [(i, index_of(*move(*coords(i)))) for i in range(X * Y * Z * CORES)]
    return lax.ppermute(array, AXES, pairs)


def z_even(z, y):
    return (z ^ 1, y)


def z_odd(z, y):
    return ((((z - 1) % Z) ^ 1) + 1) % Z, y


def y_even(z, y):
    return (z, y ^ 1)


def y_odd(z, y):
    return (z, ((((y - 1) % Y) ^ 1) + 1) % Y)


STEPS = (
    ((z_even, z_odd), (z_odd, z_even)),
    ((y_even, y_odd), (y_odd, y_even)),
)


def group_of(core, z, y):
    if core == 0:
        return [(zb, yb) for zb in sorted((z, (z + 4) % Z)) for yb in range(Y)]
    return [(zb, y) for zb in range(Z)]


GROUPS = []
for _i in range(X * Y * Z * CORES):
    _x, _y, _z, _core = coords(_i)
    _group = [index_of(_x, yb, zb, _core) for zb, yb in group_of(_core, _z, _y)]
    if _group not in GROUPS:
        GROUPS.append(_group)


def row_table():
    table = np.zeros((CORES, Z, Y, 2, 2, 192), np.int32)
    for core in range(CORES):
        for chain in range(2):
            places = [(z, y) for z in range(Z) for y in range(Y)]
            orders = {place: group_of(core, *place) for place in places}
            for step in reversed(STEPS[core][chain]):
                orders = {place: orders[place] + orders[step(*place)] for place in places}
            for (z, y), order in orders.items():
                assert len(set(order)) == Z * Y
                rows = []
                for number, (zb, yb) in enumerate(order):
                    first = (16, 8)[number % 2]
                    cut = range(first) if chain == 0 else range(first, 24)
                    rows += [(zb * Y + yb) * 48 + row for row in cut]
                table[core, z, y, 0, chain] = rows[192:]
                table[core, z, y, 1, chain] = rows[:192]
    return table.reshape(CORES * Z * Y, 1, -1)


def exchange(array, number, chain):
    def move(x, y, z, core):
        z, y = STEPS[core][chain][number](z, y)
        return (x, y, z, core)

    return permute(array, move)


def gelu_parts(preact):
    square = preact * preact
    half = 0.5 * jnp.tanh(preact * (curve_scale + (curve_scale * cubic_term) * square)) + 0.5
    values = preact * half
    slopes = half + values * (1.0 - half) * (2.0 * curve_scale + (6.0 * curve_scale * cubic_term) * square)
    return (values, slopes)


def dot(left, right, contract):
    return lax.dot_general(left, right, ((contract[:1], contract[1:]), ((), ())), preferred_element_type=jnp.float32)


VMEM = pl.BlockSpec(memory_space=pltpu.VMEM)
HBM = pl.BlockSpec(memory_space=pl.ANY)
LANES = (8, 128)


def call(kernel, name, outs, args, specs=None, scratch=(), flops=0, limit=12):
    return pl.pallas_call(
        kernel,
        out_shape=outs,
        in_specs=specs or [VMEM] * len(args),
        out_specs=jax.tree.map(lambda _: VMEM, outs),
        scratch_shapes=scratch,
        compiler_params=pltpu.CompilerParams(vmem_limit_bytes=limit * 2**20),
        cost_estimate=pl.CostEstimate(flops=flops, bytes_accessed=0, transcendentals=0),
        name=name,
    )(*args)


def array(shape, kind):
    return jax.ShapeDtypeStruct(shape, kind)


def place():
    dp, mp = lax.axis_index("dp"), lax.axis_index("mp")
    return dp // 8, (dp // 2) % 4, dp % 2, mp % 2


def mask_kernel(lengths, cotangent, out):
    positions = lax.axis_index("mp") * out.shape[1] + lax.broadcasted_iota(jnp.int32, out.shape[1:], 0)
    for e in range(out.shape[0]):
        value = cotangent[e].astype(jnp.float32)
        out[e] = jnp.where(positions < lengths[:, e : e + 1], value, 0.0).astype(out.dtype)


def load_rows(table, rows, sem):
    z, y, x_lo, core = place()
    copy = pltpu.make_async_copy(table.at[(core * Z + z) * Y + y], rows, sem)
    copy.start()
    copy.wait()
    return rows[...] + x_lo * 24


def up_kernel(table, weight, out, rows, sem):
    chosen = load_rows(table, rows, sem)
    pick = lax.broadcasted_iota(jnp.int32, (weight.shape[1], out.shape[1]), 0) == chosen
    out[...] = dot(weight[...], pick.astype(jnp.bfloat16), (1, 0)).astype(out.dtype)


def down_kernel(table, weight, out, rows, sem):
    chosen = load_rows(table, rows, sem).astype(jnp.float32)
    chosen = jnp.broadcast_to(chosen, (8, chosen.shape[1])).T[:, :1].astype(jnp.int32)
    pick = lax.broadcasted_iota(jnp.int32, (out.shape[0], weight.shape[0]), 1) == chosen
    out[...] = dot(pick.astype(jnp.bfloat16), weight[...], (1, 0)).astype(out.dtype)


def select(kernel, name, table, weight, shape, units):
    scratch = [pltpu.VMEM(table.shape[1:], jnp.int32), pltpu.SemaphoreType.DMA]
    return call(kernel, name, array(shape, weight.dtype), (table, weight), [HBM, VMEM], scratch, limit=16)


def products_of(rows, masked, up, down):
    values, slopes = gelu_parts(dot(rows, up[...], (1, 0)))
    delta = dot(masked, down[...], (1, 1)) * slopes
    return values.astype(jnp.bfloat16), delta.astype(jnp.bfloat16)


def stacked(refs, e):
    return jnp.concatenate([ref[e] for ref in refs], axis=0)


def both_examples(refs):
    return jnp.concatenate([stacked(refs, e) for e in range(2)], axis=0)


def square_of(rows, masked, hidden, delta):
    first = dot(rows, rows, (1, 1)) * dot(delta, delta, (1, 1))
    second = dot(hidden, hidden, (1, 1)) * dot(masked, masked, (1, 1))
    return jnp.broadcast_to(jnp.sum(first + second), LANES)


def early_kernel(in_a, in_b, co_a, co_b, up, down, hidden, delta):
    hidden[...], delta[...] = products_of(both_examples((in_a, in_b)), both_examples((co_a, co_b)), up, down)


def early_pass(inputs, cotans, up, down):
    out = array((4 * inputs[0].shape[1], up.shape[1]), jnp.bfloat16)
    return call(early_kernel, "early_pass", (out, out), (*inputs, *cotans, up, down))


def theirs_kernel(*refs):
    inputs, cotans = refs[:4], refs[4:8]
    up, down, hidden_out, masked_out, squares_out = refs[8:]
    for e in range(2):
        rows, masked = stacked(inputs, e), stacked(cotans, e)
        hidden, delta = products_of(rows, masked, up, down)
        hidden_out[e] = hidden.T
        masked_out[e] = masked
        squares_out[e] = square_of(rows, masked, hidden, delta)


def pass_outs(units, tokens, width, squares):
    return (
        array((2, units, tokens), jnp.bfloat16),
        array((2, tokens, width), jnp.bfloat16),
        array((squares, *LANES), jnp.float32),
    )


def theirs_pass(inputs, cotans, up, down):
    width, units = up.shape
    tokens = 4 * inputs[0].shape[1]
    return call(theirs_kernel, "theirs_pass", pass_outs(units, tokens, width, 2), (*inputs, *cotans, up, down))


def ours_kernel(*refs):
    inputs, cotans = refs[:4], refs[4:8]
    up, down, hidden_early, delta_early, theirs = refs[8:13]
    hidden_out, masked_out, squares_out = refs[13:]
    hidden_late, delta_late = products_of(both_examples(inputs[2:]), both_examples(cotans[2:]), up, down)
    half = hidden_late.shape[0] // 2
    is_first = place()[2] == 0
    for e in range(2):
        at = slice(e * half, (e + 1) * half)
        rows, masked = stacked(inputs, e), stacked(cotans, e)
        hidden = jnp.concatenate([hidden_early[at, :], hidden_late[at, :]], axis=0)
        delta = jnp.concatenate([delta_early[at, :], delta_late[at, :]], axis=0)
        hidden_out[e] = hidden.T
        masked_out[e] = masked
        square = square_of(rows, masked, hidden, delta)
        squares_out[e] = jnp.where(is_first, square, theirs[e])
        squares_out[2 + e] = jnp.where(is_first, theirs[e], square)


def ours_pass(inputs, cotans, up, down, early, theirs):
    width, units = up.shape
    tokens = 4 * inputs[0].shape[1]
    outs = pass_outs(units, tokens, width, 4)
    return call(ours_kernel, "ours_pass", outs, (*inputs, *cotans, up, down, *early, theirs))


def add_kernel(left, right, out):
    out[...] = left[...] + right[...]


def factors_of(examples, ratio, chip, across, from_left, from_right):
    total = (chip[...] + across[...]) + (from_left[...] + from_right[...])
    norms = jnp.sqrt(total)
    clip = ratio[...] * np.sqrt(np.float32(SEQ * D * FF))
    factors = clip / jnp.maximum(norms, clip)
    is_first = place()[2] == 0
    scale = jnp.where(is_first, factors, jnp.concatenate([factors[2:], factors[:2]], axis=0)) * (1.0 / examples)
    soft = jnp.floor(jax.nn.sigmoid(4.0 * (clip - norms) / clip) * 131072.0 + 0.5) * (1.0 / 131072.0)
    return scale, (soft[0] + soft[1]) + (soft[2] + soft[3])


TAIL = 16


def tail_rows(count, rows, width):
    count = count[:1, :1]
    whole = jnp.floor(count)
    rest = count - whole
    second = jnp.floor(rest * 256.0) * (1.0 / 256.0)
    rest = rest - second
    third = jnp.floor(rest * 65536.0) * (1.0 / 65536.0)
    row = lax.broadcasted_iota(jnp.int32, (8, 128), 0)
    parts = jnp.where(row == 0, whole, jnp.where(row == 1, second, jnp.where(row == 2, third, rest - third)))
    parts = jnp.where(row < 4, parts, 0.0)
    if width > 128:
        parts = jnp.concatenate([parts, jnp.zeros((8, width - 128), jnp.float32)], axis=1)
    return parts, jnp.zeros((rows - 8, width), jnp.float32)


def count_in(tail):
    return jnp.broadcast_to(jnp.sum(tail[:8, :128], axis=0, keepdims=True), LANES)


def outer_rows(at, rows, scale, operands):
    hidden_a, hidden_b, masked_a, masked_b = operands
    total = None
    for e in range(4):
        hidden, masked = ((hidden_a, masked_a), (hidden_b, masked_b))[e // 2]
        piece = scale[e, :1, :1] * dot(hidden[e % 2, at : at + rows, :], masked[e % 2], (1, 0))
        total = piece if total is None else total + piece
    return total


def outer_send_kernel(examples, *refs):
    small, operands, (out0, out1, count_out, scale_out) = refs[:5], refs[5:9], refs[9:]
    rows, width = out1.shape
    scale, count = factors_of(examples, *small)
    count_out[...] = count
    scale_out[...] = scale
    total = outer_rows(0, rows, scale, operands)
    out0[...] = jnp.concatenate([total, *tail_rows(count, TAIL, width)], axis=0).astype(out0.dtype)
    out1[...] = outer_rows(rows, rows, scale, operands).astype(out1.dtype)


def outer_keep_kernel(scale, *refs):
    operands, outs = refs[:4], refs[4:]
    rows = outs[0].shape[0]
    for chain, out in enumerate(outs):
        out[...] = outer_rows((2 + chain) * rows, rows, scale[...], operands)


def outer_send(rows, examples, small, operands):
    width = operands[2].shape[2]
    outs = (
        array((rows + TAIL, width), jnp.bfloat16),
        array((rows, width), jnp.bfloat16),
        array(LANES, jnp.float32),
        array((4, *LANES), jnp.float32),
    )
    return call(lambda *refs: outer_send_kernel(examples, *refs), "outer_send", outs, (*small, *operands))


def outer_keep(rows, scale, operands):
    outs = (array((rows, operands[2].shape[2]), jnp.float32),) * 2
    return call(outer_keep_kernel, "outer_keep", outs, (scale, *operands))


def step_first_kernel(count, kept, got, count_out, keep, send):
    rows, width = kept.shape
    half = rows // 2
    message = got[...].astype(jnp.float32)
    total = kept[...] + message[:rows]
    keep[...] = total[:half]
    counted = count[...] + count_in(message[rows:])
    count_out[...] = counted
    send[...] = jnp.concatenate([total[half:], *tail_rows(counted, TAIL, width)], axis=0).astype(send.dtype)


def step_outs(kept, sent, width):
    return (array(LANES, jnp.float32), array((kept, width), jnp.float32), array((sent, width), jnp.bfloat16))


def step_first(count, kept, got):
    rows, width = kept.shape
    return call(step_first_kernel, "step_first", step_outs(rows // 2, rows // 2 + TAIL, width), (count, kept, got))


def step_second_kernel(kept, got, keep, send):
    half = kept.shape[0] // 2
    total = kept[...] + got[...].astype(jnp.float32)
    keep[...] = total[:half]
    send[...] = total[half:].astype(send.dtype)


def step_second(kept, got):
    rows, width = kept.shape
    outs = (array((rows // 2, width), jnp.float32), array((rows // 2, width), jnp.bfloat16))
    return call(step_second_kernel, "step_second", outs, (kept, got))


SIDE = 128


def step_join_kernel(count, kept0, kept1, got0, got1, send):
    rows, width = kept0.shape
    message = got0[...].astype(jnp.float32)
    total0 = kept0[...] + message[:rows]
    total1 = kept1[...] + got1[...].astype(jnp.float32)
    counted = count[...] + count_in(message[rows:])
    pieces = []
    for at in range(0, rows, 24):
        pieces += [total0[at : at + 16], total1[at : at + 8], total0[at + 16 : at + 24], total1[at + 8 : at + 24]]
    side = tail_rows(counted, 24, SIDE)
    side = jnp.concatenate(list(side) * (rows // 12), axis=0)
    send[...] = jnp.concatenate([jnp.concatenate(pieces, axis=0), side], axis=1).astype(send.dtype)


def step_join(count, kept0, kept1, got0, got1):
    rows, width = kept0.shape
    return call(step_join_kernel, "step_join", array((2 * rows, width + SIDE), jnp.bfloat16), (count, kept0, kept1, got0, got1))


def step_last_kernel(examples, ratio, noise, got, out, ratio_next):
    rows, width = out.shape
    message = got[...].astype(jnp.float32)
    chunks = [message[at : at + rows] for at in range(0, message.shape[0], rows)]
    while len(chunks) > 1:
        chunks = [a + b for a, b in zip(chunks[::2], chunks[1::2])]
    out[...] = chunks[0][:, :width]
    count = jnp.sum(chunks[0][:8, width:], axis=0, keepdims=True)
    share = (count[:, :1] + noise[...]) / examples
    ratio_next[...] = ratio[...] * jnp.exp(-(share - target_share))


def step_last(examples, ratio, noise, got, rows, width):
    outs = (array((rows, width), jnp.float32), array((1, 1), jnp.float32))
    args = (ratio.reshape(1, 1), noise.reshape(1, 1), got)
    return call(lambda *refs: step_last_kernel(examples, *refs), "step_last", outs, args)


def right(x, y, z, core):
    return (x + 1, y, z, core)


def left(x, y, z, core):
    return (x - 1, y, z, core)


def other_core(x, y, z, core):
    return (x, y, z, 1 - core)


def opposite(x, y, z, core):
    return (x + 2, y, z, core)


def swap_cores(*arrays):
    return [permute(array, other_core) for array in arrays]


def after(array, *others):
    return lax.optimization_barrier((array, *others))[0]


def per_device(inputs, cotangent, lengths, up_weight, down_weight, clip_ratio, count_noise):
    in_l = permute(inputs, right)
    masked = call(
        mask_kernel, "mask", array(cotangent.shape, cotangent.dtype), (lengths.reshape(1, -1), cotangent)
    )
    co_r = permute(masked, left)

    table = jnp.asarray(row_table())
    width, units = up_weight.shape
    up = select(up_kernel, "select_up", table, up_weight, (width, units // 2), units // 2)
    down = select(down_kernel, "select_down", table, down_weight, (units // 2, width), units // 2)

    in_s, co_s = swap_cores(inputs, masked)
    co_l = permute(masked, right)
    in_r = permute(inputs, left)
    early = early_pass((inputs, in_s), (masked, co_s), up, down)
    ratio = permute(after(clip_ratio.reshape(1, 1), up, down), other_core)
    in_l, in_r, co_l, co_r = (after(part, ratio) for part in (in_l, in_r, co_l, co_r))
    in_o = permute(in_l, right)
    co_o = permute(co_r, left)
    in_ls, in_rs, co_ls, co_rs = swap_cores(in_l, in_r, co_l, co_r)
    hidden_theirs, masked_theirs, squares_theirs = theirs_pass(
        (in_l, in_ls, in_r, in_rs), (co_l, co_ls, co_r, co_rs), *after((up, down), *early)
    )
    in_os, co_os = swap_cores(after(in_o, squares_theirs), after(co_o, squares_theirs))
    hidden_ours, masked_ours, squares = ours_pass(
        (inputs, in_s, in_o, in_os), (masked, co_s, co_o, co_os), up, down, early, squares_theirs
    )

    chip = call(add_kernel, "chip_squares", array(squares.shape, squares.dtype), (squares, permute(squares, other_core)))
    small = (ratio, chip, *(permute(chip, move) for move in (opposite, right, left)))
    examples_all = lax.axis_size("dp") * lengths.shape[0]
    operands = (hidden_ours, hidden_theirs, masked_ours, masked_theirs)
    quarter = units // 8
    send0, send1, count, scale = outer_send(quarter, examples_all, small, operands)
    got0, got1 = exchange(send0, 0, 0), exchange(send1, 0, 1)
    keep0, keep1 = outer_keep(quarter, scale, operands)
    count, keep0, send0 = step_first(count, keep0, got0)
    got0 = exchange(send0, 1, 0)
    keep1, send1 = step_second(keep1, got1)
    got1 = exchange(send1, 1, 1)
    send = step_join(count, keep0, keep1, got0, got1)
    got = lax.all_to_all(send, AXES, 0, 0, axis_index_groups=GROUPS, tiled=True)
    grad_down, ratio_next = step_last(
        examples_all, ratio, count_noise, got, 4 * quarter // (Z * Y), send.shape[1] - SIDE
    )
    return (grad_down, ratio_next.reshape(1))


def solution(mesh):
    return jax.shard_map(
        per_device,
        mesh=mesh,
        in_specs=(
            P("dp", "mp", None),
            P("dp", "mp", None),
            P("dp"),
            P(None, "mp"),
            P("mp", None),
            P(),
            P(),
        ),
        out_specs=(P(("mp", "dp"), None), P()),
        check_vma=False,
    )
```

```python
import jax
import jax.numpy as jnp
import numpy as np
from jax import lax
from jax.experimental import pallas as pl
from jax.experimental.pallas import tpu as pltpu
from jax.sharding import PartitionSpec as P

D = 1152
FF = 6144
SEQ = 256
AXES = ("dp", "mp")

curve_scale = 0.7978845608028654
cubic_term = 0.044715
target_share = 0.5

X, Y, Z, CORES = 4, 4, 8, 2


def coords(i):
    dp, mp = divmod(i, 4)
    z, rest = divmod(dp, 8)
    y, x_lo = divmod(rest, 2)
    x_hi, core = divmod(mp, 2)
    return (x_hi * 2 + x_lo, y, z, core)


def index_of(x, y, z, core):
    x, y, z = x % X, y % Y, z % Z
    return (z * 8 + y * 2 + x % 2) * 4 + (x // 2) * 2 + core


def permute(array, move):
    pairs = [(i, index_of(*move(*coords(i)))) for i in range(X * Y * Z * CORES)]
    return lax.ppermute(array, AXES, pairs)


def z_even(z, y):
    return (z ^ 1, y)


def z_odd(z, y):
    return ((((z - 1) % Z) ^ 1) + 1) % Z, y


def y_even(z, y):
    return (z, y ^ 1)


def y_odd(z, y):
    return (z, ((((y - 1) % Y) ^ 1) + 1) % Y)


STEPS = (
    ((z_even, z_odd), (z_odd, z_even)),
    ((y_even, y_odd), (y_odd, y_even)),
)


def group_of(core, z, y):
    if core == 0:
        return [(zb, yb) for zb in sorted((z, (z + 4) % Z)) for yb in range(Y)]
    return [(zb, y) for zb in range(Z)]


GROUPS = []
for _i in range(X * Y * Z * CORES):
    _x, _y, _z, _core = coords(_i)
    _group = [index_of(_x, yb, zb, _core) for zb, yb in group_of(_core, _z, _y)]
    if _group not in GROUPS:
        GROUPS.append(_group)


def row_table():
    table = np.zeros((CORES, Z, Y, 2, 2, 192), np.int32)
    for core in range(CORES):
        for chain in range(2):
            places = [(z, y) for z in range(Z) for y in range(Y)]
            orders = {place: group_of(core, *place) for place in places}
            for step in reversed(STEPS[core][chain]):
                orders = {place: orders[place] + orders[step(*place)] for place in places}
            for (z, y), order in orders.items():
                assert len(set(order)) == Z * Y
                rows = []
                for number, (zb, yb) in enumerate(order):
                    first = (16, 8)[number % 2]
                    cut = range(first) if chain == 0 else range(first, 24)
                    rows += [(zb * Y + yb) * 48 + row for row in cut]
                table[core, z, y, 0, chain] = rows[192:]
                table[core, z, y, 1, chain] = rows[:192]
    return table.reshape(CORES * Z * Y, 1, -1)


def exchange(array, number, chain):
    def move(x, y, z, core):
        z, y = STEPS[core][chain][number](z, y)
        return (x, y, z, core)

    return permute(array, move)


def gelu_parts(preact):
    square = preact * preact
    half = 0.5 * jnp.tanh(preact * (curve_scale + (curve_scale * cubic_term) * square)) + 0.5
    values = preact * half
    slopes = half + values * (1.0 - half) * (2.0 * curve_scale + (6.0 * curve_scale * cubic_term) * square)
    return (values, slopes)


def dot(left, right, contract):
    return lax.dot_general(left, right, ((contract[:1], contract[1:]), ((), ())), preferred_element_type=jnp.float32)


VMEM = pl.BlockSpec(memory_space=pltpu.VMEM)
HBM = pl.BlockSpec(memory_space=pl.ANY)
LANES = (8, 128)


def call(kernel, name, outs, args, specs=None, scratch=(), flops=0, limit=12):
    return pl.pallas_call(
        kernel,
        out_shape=outs,
        in_specs=specs or [VMEM] * len(args),
        out_specs=jax.tree.map(lambda _: VMEM, outs),
        scratch_shapes=scratch,
        compiler_params=pltpu.CompilerParams(vmem_limit_bytes=limit * 2**20),
        cost_estimate=pl.CostEstimate(flops=flops, bytes_accessed=0, transcendentals=0),
        name=name,
    )(*args)


def array(shape, kind):
    return jax.ShapeDtypeStruct(shape, kind)


def place():
    dp, mp = lax.axis_index("dp"), lax.axis_index("mp")
    return dp // 8, (dp // 2) % 4, dp % 2, mp % 2


def mask_kernel(lengths, cotangent, out):
    positions = lax.axis_index("mp") * out.shape[1] + lax.broadcasted_iota(jnp.int32, out.shape[1:], 0)
    for e in range(out.shape[0]):
        value = cotangent[e].astype(jnp.float32)
        out[e] = jnp.where(positions < lengths[:, e : e + 1], value, 0.0).astype(out.dtype)


def load_rows(table, rows, sem):
    z, y, x_lo, core = place()
    copy = pltpu.make_async_copy(table.at[(core * Z + z) * Y + y], rows, sem)
    copy.start()
    copy.wait()
    return rows[...] + x_lo * 24


def up_kernel(table, weight, out, rows, sem):
    chosen = load_rows(table, rows, sem)
    pick = lax.broadcasted_iota(jnp.int32, (weight.shape[1], out.shape[1]), 0) == chosen
    out[...] = dot(weight[...], pick.astype(jnp.bfloat16), (1, 0)).astype(out.dtype)


def down_kernel(table, weight, out, rows, sem):
    chosen = load_rows(table, rows, sem).astype(jnp.float32)
    chosen = jnp.broadcast_to(chosen, (8, chosen.shape[1])).T[:, :1].astype(jnp.int32)
    pick = lax.broadcasted_iota(jnp.int32, (out.shape[0], weight.shape[0]), 1) == chosen
    out[...] = dot(pick.astype(jnp.bfloat16), weight[...], (1, 0)).astype(out.dtype)


def select(kernel, name, table, weight, shape, units):
    scratch = [pltpu.VMEM(table.shape[1:], jnp.int32), pltpu.SemaphoreType.DMA]
    return call(kernel, name, array(shape, weight.dtype), (table, weight), [HBM, VMEM], scratch, limit=16)


def products_of(rows, masked, up, down):
    values, slopes = gelu_parts(dot(rows, up[...], (1, 0)))
    delta = dot(masked, down[...], (1, 1)) * slopes
    return values.astype(jnp.bfloat16), delta.astype(jnp.bfloat16)


def stacked(refs, e):
    return jnp.concatenate([ref[e] for ref in refs], axis=0)


def both_examples(refs):
    return jnp.concatenate([stacked(refs, e) for e in range(2)], axis=0)


def square_of(rows, masked, hidden, delta):
    first = dot(rows, rows, (1, 1)) * dot(delta, delta, (1, 1))
    second = dot(hidden, hidden, (1, 1)) * dot(masked, masked, (1, 1))
    return jnp.broadcast_to(jnp.sum(first + second), LANES)


def early_kernel(in_a, in_b, co_a, co_b, up, down, hidden, delta):
    hidden[...], delta[...] = products_of(both_examples((in_a, in_b)), both_examples((co_a, co_b)), up, down)


def early_pass(inputs, cotans, up, down):
    out = array((4 * inputs[0].shape[1], up.shape[1]), jnp.bfloat16)
    return call(early_kernel, "early_pass", (out, out), (*inputs, *cotans, up, down))


def theirs_kernel(*refs):
    inputs, cotans = refs[:4], refs[4:8]
    up, down, hidden_out, masked_out, squares_out = refs[8:]
    for e in range(2):
        rows, masked = stacked(inputs, e), stacked(cotans, e)
        hidden, delta = products_of(rows, masked, up, down)
        hidden_out[e] = hidden.T
        masked_out[e] = masked
        squares_out[e] = square_of(rows, masked, hidden, delta)


def pass_outs(units, tokens, width, squares):
    return (
        array((2, units, tokens), jnp.bfloat16),
        array((2, tokens, width), jnp.bfloat16),
        array((squares, *LANES), jnp.float32),
    )


def theirs_pass(inputs, cotans, up, down):
    width, units = up.shape
    tokens = 4 * inputs[0].shape[1]
    return call(theirs_kernel, "theirs_pass", pass_outs(units, tokens, width, 2), (*inputs, *cotans, up, down))


def ours_kernel(*refs):
    inputs, cotans = refs[:4], refs[4:8]
    up, down, hidden_early, delta_early, theirs = refs[8:13]
    hidden_out, masked_out, squares_out = refs[13:]
    hidden_late, delta_late = products_of(both_examples(inputs[2:]), both_examples(cotans[2:]), up, down)
    half = hidden_late.shape[0] // 2
    is_first = place()[2] == 0
    for e in range(2):
        at = slice(e * half, (e + 1) * half)
        rows, masked = stacked(inputs, e), stacked(cotans, e)
        hidden = jnp.concatenate([hidden_early[at, :], hidden_late[at, :]], axis=0)
        delta = jnp.concatenate([delta_early[at, :], delta_late[at, :]], axis=0)
        hidden_out[e] = hidden.T
        masked_out[e] = masked
        square = square_of(rows, masked, hidden, delta)
        squares_out[e] = jnp.where(is_first, square, theirs[e])
        squares_out[2 + e] = jnp.where(is_first, theirs[e], square)


def ours_pass(inputs, cotans, up, down, early, theirs):
    width, units = up.shape
    tokens = 4 * inputs[0].shape[1]
    outs = pass_outs(units, tokens, width, 4)
    return call(ours_kernel, "ours_pass", outs, (*inputs, *cotans, up, down, *early, theirs))


def add_kernel(left, right, out):
    out[...] = left[...] + right[...]


def factors_of(examples, ratio, chip, across, from_left, from_right):
    total = (chip[...] + across[...]) + (from_left[...] + from_right[...])
    norms = jnp.sqrt(total)
    clip = ratio[...] * np.sqrt(np.float32(SEQ * D * FF))
    factors = clip / jnp.maximum(norms, clip)
    is_first = place()[2] == 0
    scale = jnp.where(is_first, factors, jnp.concatenate([factors[2:], factors[:2]], axis=0)) * (1.0 / examples)
    soft = jnp.floor(jax.nn.sigmoid(4.0 * (clip - norms) / clip) * 131072.0 + 0.5) * (1.0 / 131072.0)
    return scale, (soft[0] + soft[1]) + (soft[2] + soft[3])


TAIL = 16


def tail_rows(count, rows, width):
    count = count[:1, :1]
    whole = jnp.floor(count)
    rest = count - whole
    second = jnp.floor(rest * 256.0) * (1.0 / 256.0)
    rest = rest - second
    third = jnp.floor(rest * 65536.0) * (1.0 / 65536.0)
    row = lax.broadcasted_iota(jnp.int32, (8, 128), 0)
    parts = jnp.where(row == 0, whole, jnp.where(row == 1, second, jnp.where(row == 2, third, rest - third)))
    parts = jnp.where(row < 4, parts, 0.0)
    if width > 128:
        parts = jnp.concatenate([parts, jnp.zeros((8, width - 128), jnp.float32)], axis=1)
    return parts, jnp.zeros((rows - 8, width), jnp.float32)


def count_in(tail):
    return jnp.broadcast_to(jnp.sum(tail[:8, :128], axis=0, keepdims=True), LANES)


def outer_rows(at, rows, scale, operands):
    hidden_a, hidden_b, masked_a, masked_b = operands
    total = None
    for e in range(4):
        hidden, masked = ((hidden_a, masked_a), (hidden_b, masked_b))[e // 2]
        piece = scale[e, :1, :1] * dot(hidden[e % 2, at : at + rows, :], masked[e % 2], (1, 0))
        total = piece if total is None else total + piece
    return total


def outer_first_kernel(examples, *refs):
    small, operands, (out, count_out, scale_out) = refs[:5], refs[5:9], refs[9:]
    rows, width = out.shape[0] - TAIL, out.shape[1]
    scale, count = factors_of(examples, *small)
    count_out[...] = count
    scale_out[...] = scale
    total = outer_rows(0, rows, scale, operands)
    out[...] = jnp.concatenate([total, *tail_rows(count, TAIL, width)], axis=0).astype(out.dtype)


def outer_second_kernel(scale, *refs):
    operands, out = refs[:4], refs[4]
    rows = out.shape[0]
    out[...] = outer_rows(rows, rows, scale[...], operands).astype(out.dtype)


def outer_keep_kernel(scale, *refs):
    operands, outs = refs[:4], refs[4:]
    rows = outs[0].shape[0]
    for chain, out in enumerate(outs):
        out[...] = outer_rows((2 + chain) * rows, rows, scale[...], operands)


def outer_first(rows, examples, small, operands):
    outs = (
        array((rows + TAIL, operands[2].shape[2]), jnp.bfloat16),
        array(LANES, jnp.float32),
        array((4, *LANES), jnp.float32),
    )
    return call(lambda *refs: outer_first_kernel(examples, *refs), "outer_first", outs, (*small, *operands))


def outer_second(rows, scale, operands):
    out = array((rows, operands[2].shape[2]), jnp.bfloat16)
    return call(outer_second_kernel, "outer_second", out, (scale, *operands))


def outer_keep(rows, scale, operands):
    outs = (array((rows, operands[2].shape[2]), jnp.float32),) * 2
    return call(outer_keep_kernel, "outer_keep", outs, (scale, *operands))


def step_first_kernel(count, kept, got, count_out, keep, send):
    rows, width = kept.shape
    half = rows // 2
    message = got[...].astype(jnp.float32)
    total = kept[...] + message[:rows]
    keep[...] = total[:half]
    counted = count[...] + count_in(message[rows:])
    count_out[...] = counted
    send[...] = jnp.concatenate([total[half:], *tail_rows(counted, TAIL, width)], axis=0).astype(send.dtype)


def step_outs(kept, sent, width):
    return (array(LANES, jnp.float32), array((kept, width), jnp.float32), array((sent, width), jnp.bfloat16))


def step_first(count, kept, got):
    rows, width = kept.shape
    return call(step_first_kernel, "step_first", step_outs(rows // 2, rows // 2 + TAIL, width), (count, kept, got))


def step_second_kernel(kept, got, keep, send):
    half = kept.shape[0] // 2
    total = kept[...] + got[...].astype(jnp.float32)
    keep[...] = total[:half]
    send[...] = total[half:].astype(send.dtype)


def step_second(kept, got):
    rows, width = kept.shape
    outs = (array((rows // 2, width), jnp.float32), array((rows // 2, width), jnp.bfloat16))
    return call(step_second_kernel, "step_second", outs, (kept, got))


SIDE = 128


def step_join_kernel(count, kept0, kept1, got0, got1, send):
    rows, width = kept0.shape
    message = got0[...].astype(jnp.float32)
    total0 = kept0[...] + message[:rows]
    total1 = kept1[...] + got1[...].astype(jnp.float32)
    counted = count[...] + count_in(message[rows:])
    pieces = []
    for at in range(0, rows, 24):
        pieces += [total0[at : at + 16], total1[at : at + 8], total0[at + 16 : at + 24], total1[at + 8 : at + 24]]
    side = tail_rows(counted, 24, SIDE)
    side = jnp.concatenate(list(side) * (rows // 12), axis=0)
    send[...] = jnp.concatenate([jnp.concatenate(pieces, axis=0), side], axis=1).astype(send.dtype)


def step_join(count, kept0, kept1, got0, got1):
    rows, width = kept0.shape
    return call(step_join_kernel, "step_join", array((2 * rows, width + SIDE), jnp.bfloat16), (count, kept0, kept1, got0, got1))


def step_last_kernel(examples, ratio, noise, got, out, ratio_next):
    rows, width = out.shape
    message = got[...].astype(jnp.float32)
    chunks = [message[at : at + rows] for at in range(0, message.shape[0], rows)]
    while len(chunks) > 1:
        chunks = [a + b for a, b in zip(chunks[::2], chunks[1::2])]
    out[...] = chunks[0][:, :width]
    count = jnp.sum(chunks[0][:8, width:], axis=0, keepdims=True)
    share = (count[:, :1] + noise[...]) / examples
    ratio_next[...] = ratio[...] * jnp.exp(-(share - target_share))


def step_last(examples, ratio, noise, got, rows, width):
    outs = (array((rows, width), jnp.float32), array((1, 1), jnp.float32))
    args = (ratio.reshape(1, 1), noise.reshape(1, 1), got)
    return call(lambda *refs: step_last_kernel(examples, *refs), "step_last", outs, args)


def right(x, y, z, core):
    return (x + 1, y, z, core)


def left(x, y, z, core):
    return (x - 1, y, z, core)


def other_core(x, y, z, core):
    return (x, y, z, 1 - core)


def opposite(x, y, z, core):
    return (x + 2, y, z, core)


def swap_cores(*arrays):
    return [permute(array, other_core) for array in arrays]


def after(array, *others):
    return lax.optimization_barrier((array, *others))[0]


def per_device(inputs, cotangent, lengths, up_weight, down_weight, clip_ratio, count_noise):
    in_l = permute(inputs, right)
    masked = call(
        mask_kernel, "mask", array(cotangent.shape, cotangent.dtype), (lengths.reshape(1, -1), cotangent), flops=5 * 10**9
    )
    co_r = permute(masked, left)

    table = jnp.asarray(row_table())
    width, units = up_weight.shape
    up = select(up_kernel, "select_up", table, up_weight, (width, units // 2), units // 2)
    down = select(down_kernel, "select_down", table, down_weight, (units // 2, width), units // 2)

    in_s, co_s = swap_cores(inputs, masked)
    co_l = permute(masked, right)
    in_r = permute(inputs, left)
    early = early_pass((inputs, in_s), (masked, co_s), up, down)
    ratio = permute(after(clip_ratio.reshape(1, 1), up, down), other_core)
    in_l, in_r, co_l, co_r = (after(part, ratio) for part in (in_l, in_r, co_l, co_r))
    in_o = permute(in_l, right)
    co_o = permute(co_r, left)
    in_ls, in_rs, co_ls, co_rs = swap_cores(in_l, in_r, co_l, co_r)
    hidden_theirs, masked_theirs, squares_theirs = theirs_pass(
        (in_l, in_ls, in_r, in_rs), (co_l, co_ls, co_r, co_rs), *after((up, down), *early)
    )
    in_os, co_os = swap_cores(after(in_o, squares_theirs), after(co_o, squares_theirs))
    hidden_ours, masked_ours, squares = ours_pass(
        (inputs, in_s, in_o, in_os), (masked, co_s, co_o, co_os), up, down, early, squares_theirs
    )

    chip = call(add_kernel, "chip_squares", array(squares.shape, squares.dtype), (squares, permute(squares, other_core)))
    small = (ratio, chip, *(permute(chip, move) for move in (opposite, right, left)))
    examples_all = lax.axis_size("dp") * lengths.shape[0]
    operands = (hidden_ours, hidden_theirs, masked_ours, masked_theirs)
    quarter = units // 8
    send0, count, scale = outer_first(quarter, examples_all, small, operands)
    send1 = outer_second(quarter, scale, operands)
    got0, got1 = exchange(send0, 0, 0), exchange(send1, 0, 1)
    keep0, keep1 = outer_keep(quarter, scale, operands)
    count, keep0, send0 = step_first(count, keep0, got0)
    got0 = exchange(send0, 1, 0)
    keep1, send1 = step_second(keep1, got1)
    got1 = exchange(send1, 1, 1)
    send = step_join(count, keep0, keep1, got0, got1)
    got = lax.all_to_all(send, AXES, 0, 0, axis_index_groups=GROUPS, tiled=True)
    grad_down, ratio_next = step_last(
        examples_all, ratio, count_noise, got, 4 * quarter // (Z * Y), send.shape[1] - SIDE
    )
    return (grad_down, ratio_next.reshape(1))


def solution(mesh):
    return jax.shard_map(
        per_device,
        mesh=mesh,
        in_specs=(
            P("dp", "mp", None),
            P("dp", "mp", None),
            P("dp"),
            P(None, "mp"),
            P("mp", None),
            P(),
            P(),
        ),
        out_specs=(P(("mp", "dp"), None), P()),
        check_vma=False,
    )
```

```python
import jax
import jax.numpy as jnp
import numpy as np
from jax import lax
from jax.experimental import pallas as pl
from jax.experimental.pallas import tpu as pltpu
from jax.sharding import PartitionSpec as P

D = 1152
FF = 6144
SEQ = 256
AXES = ("dp", "mp")

curve_scale = 0.7978845608028654
cubic_term = 0.044715
target_share = 0.5

X, Y, Z, CORES = 4, 4, 8, 2


def coords(i):
    dp, mp = divmod(i, 4)
    z, rest = divmod(dp, 8)
    y, x_lo = divmod(rest, 2)
    x_hi, core = divmod(mp, 2)
    return (x_hi * 2 + x_lo, y, z, core)


def index_of(x, y, z, core):
    x, y, z = x % X, y % Y, z % Z
    return (z * 8 + y * 2 + x % 2) * 4 + (x // 2) * 2 + core


def permute(array, move):
    pairs = [(i, index_of(*move(*coords(i)))) for i in range(X * Y * Z * CORES)]
    return lax.ppermute(array, AXES, pairs)


def partners(core, z, y):
    if core == 0:
        return (((z + 1) % Z, y), ((z - 1) % Z, y), ((z + (2 if z % 4 < 2 else -2)) % Z, y))
    return ((z, (y + 1) % Y), (z, (y - 1) % Y), (z, (y + 2) % Y))


def group_of(core, z, y):
    if core == 0:
        return [(zb, yb) for zb in (z % 4, z % 4 + 4) for yb in range(Y)]
    return [(zb, y) for zb in range(Z)]


GROUPS = []
for _i in range(X * Y * Z * CORES):
    _x, _y, _z, _core = coords(_i)
    _group = [index_of(_x, yb, zb, _core) for zb, yb in group_of(_core, _z, _y)]
    if _group not in GROUPS:
        GROUPS.append(_group)


def row_table():
    table = np.zeros((CORES, Z, Y, 32 * 24), np.int32)
    for core in range(CORES):
        for z in range(Z):
            for y in range(Y):
                blocks = [block for place in (*partners(core, z, y), (z, y)) for block in group_of(core, *place)]
                assert len(set(blocks)) == Z * Y
                table[core, z, y] = [(zb * Y + yb) * 48 + row for zb, yb in blocks for row in range(24)]
    return table.reshape(CORES * Z * Y, 1, -1)


def exchange(array, number):
    def move(x, y, z, core):
        z, y = partners(core, z, y)[number]
        return (x, y, z, core)

    return permute(array, move)


def gelu_parts(preact):
    square = preact * preact
    half = 0.5 * jnp.tanh(preact * (curve_scale + (curve_scale * cubic_term) * square)) + 0.5
    values = preact * half
    slopes = half + values * (1.0 - half) * (2.0 * curve_scale + (6.0 * curve_scale * cubic_term) * square)
    return (values, slopes)


def dot(left, right, contract):
    return lax.dot_general(left, right, ((contract[:1], contract[1:]), ((), ())), preferred_element_type=jnp.float32)


VMEM = pl.BlockSpec(memory_space=pltpu.VMEM)
HBM = pl.BlockSpec(memory_space=pl.ANY)
LANES = (8, 128)


def call(kernel, name, outs, args, specs=None, scratch=(), flops=0, limit=12):
    return pl.pallas_call(
        kernel,
        out_shape=outs,
        in_specs=specs or [VMEM] * len(args),
        out_specs=jax.tree.map(lambda _: VMEM, outs),
        scratch_shapes=scratch,
        compiler_params=pltpu.CompilerParams(vmem_limit_bytes=limit * 2**20),
        cost_estimate=pl.CostEstimate(flops=flops, bytes_accessed=0, transcendentals=0),
        name=name,
    )(*args)


def array(shape, kind):
    return jax.ShapeDtypeStruct(shape, kind)


def place():
    dp, mp = lax.axis_index("dp"), lax.axis_index("mp")
    return dp // 8, (dp // 2) % 4, dp % 2, mp % 2


def mask_kernel(lengths, cotangent, out):
    positions = lax.axis_index("mp") * out.shape[1] + lax.broadcasted_iota(jnp.int32, out.shape[1:], 0)
    for e in range(out.shape[0]):
        value = cotangent[e].astype(jnp.float32)
        out[e] = jnp.where(positions < lengths[:, e : e + 1], value, 0.0).astype(out.dtype)


def load_rows(table, rows, sem):
    z, y, x_lo, core = place()
    copy = pltpu.make_async_copy(table.at[(core * Z + z) * Y + y], rows, sem)
    copy.start()
    copy.wait()
    return rows[...] + x_lo * 24


def up_kernel(table, weight, out, rows, sem):
    chosen = load_rows(table, rows, sem)
    pick = lax.broadcasted_iota(jnp.int32, (weight.shape[1], out.shape[1]), 0) == chosen
    out[...] = dot(weight[...], pick.astype(jnp.bfloat16), (1, 0)).astype(out.dtype)


def down_kernel(table, weight, out, rows, sem):
    chosen = load_rows(table, rows, sem).astype(jnp.float32)
    chosen = jnp.broadcast_to(chosen, (8, chosen.shape[1])).T[:, :1].astype(jnp.int32)
    pick = lax.broadcasted_iota(jnp.int32, (out.shape[0], weight.shape[0]), 1) == chosen
    out[...] = dot(pick.astype(jnp.bfloat16), weight[...], (1, 0)).astype(out.dtype)


def select(kernel, name, table, weight, shape, units):
    scratch = [pltpu.VMEM(table.shape[1:], jnp.int32), pltpu.SemaphoreType.DMA]
    return call(kernel, name, array(shape, weight.dtype), (table, weight), [HBM, VMEM], scratch, limit=16)


def products_of(rows, masked, up, down):
    values, slopes = gelu_parts(dot(rows, up[...], (1, 0)))
    delta = dot(masked, down[...], (1, 1)) * slopes
    return values.astype(jnp.bfloat16), delta.astype(jnp.bfloat16)


def stacked(refs, e):
    return jnp.concatenate([ref[e] for ref in refs], axis=0)


def both_examples(refs):
    return jnp.concatenate([stacked(refs, e) for e in range(2)], axis=0)


def square_of(rows, masked, hidden, delta):
    first = dot(rows, rows, (1, 1)) * dot(delta, delta, (1, 1))
    second = dot(hidden, hidden, (1, 1)) * dot(masked, masked, (1, 1))
    return jnp.broadcast_to(jnp.sum(first + second), LANES)


def early_kernel(in_a, in_b, co_a, co_b, up, down, hidden, delta):
    hidden[...], delta[...] = products_of(both_examples((in_a, in_b)), both_examples((co_a, co_b)), up, down)


def early_pass(inputs, cotans, up, down):
    out = array((4 * inputs[0].shape[1], up.shape[1]), jnp.bfloat16)
    return call(early_kernel, "early_pass", (out, out), (*inputs, *cotans, up, down))


def theirs_kernel(*refs):
    inputs, cotans = refs[:4], refs[4:8]
    up, down, hidden_out, masked_out, squares_out = refs[8:]
    for e in range(2):
        rows, masked = stacked(inputs, e), stacked(cotans, e)
        hidden, delta = products_of(rows, masked, up, down)
        hidden_out[e] = hidden.T
        masked_out[e] = masked
        squares_out[e] = square_of(rows, masked, hidden, delta)


def pass_outs(units, tokens, width, squares):
    return (
        array((2, units, tokens), jnp.bfloat16),
        array((2, tokens, width), jnp.bfloat16),
        array((squares, *LANES), jnp.float32),
    )


def theirs_pass(inputs, cotans, up, down):
    width, units = up.shape
    tokens = 4 * inputs[0].shape[1]
    return call(theirs_kernel, "theirs_pass", pass_outs(units, tokens, width, 2), (*inputs, *cotans, up, down))


def ours_kernel(*refs):
    inputs, cotans = refs[:4], refs[4:8]
    up, down, hidden_early, delta_early, theirs = refs[8:13]
    hidden_out, masked_out, squares_out = refs[13:]
    hidden_late, delta_late = products_of(both_examples(inputs[2:]), both_examples(cotans[2:]), up, down)
    half = hidden_late.shape[0] // 2
    is_first = place()[2] == 0
    for e in range(2):
        at = slice(e * half, (e + 1) * half)
        rows, masked = stacked(inputs, e), stacked(cotans, e)
        hidden = jnp.concatenate([hidden_early[at, :], hidden_late[at, :]], axis=0)
        delta = jnp.concatenate([delta_early[at, :], delta_late[at, :]], axis=0)
        hidden_out[e] = hidden.T
        masked_out[e] = masked
        square = square_of(rows, masked, hidden, delta)
        squares_out[e] = jnp.where(is_first, square, theirs[e])
        squares_out[2 + e] = jnp.where(is_first, theirs[e], square)


def ours_pass(inputs, cotans, up, down, early, theirs):
    width, units = up.shape
    tokens = 4 * inputs[0].shape[1]
    outs = pass_outs(units, tokens, width, 4)
    return call(ours_kernel, "ours_pass", outs, (*inputs, *cotans, up, down, *early, theirs))


def add_kernel(left, right, out):
    out[...] = left[...] + right[...]


def factors_of(examples, ratio, chip, across, from_left, from_right):
    total = (chip[...] + across[...]) + (from_left[...] + from_right[...])
    norms = jnp.sqrt(total)
    clip = ratio[...] * np.sqrt(np.float32(SEQ * D * FF))
    factors = clip / jnp.maximum(norms, clip)
    is_first = place()[2] == 0
    scale = jnp.where(is_first, factors, jnp.concatenate([factors[2:], factors[:2]], axis=0)) * (1.0 / examples)
    soft = jnp.floor(jax.nn.sigmoid(4.0 * (clip - norms) / clip) * 131072.0 + 0.5) * (1.0 / 131072.0)
    return scale, (soft[0] + soft[1]) + (soft[2] + soft[3])


TAIL = 16


def tail_rows(count, rows, width):
    count = count[:1, :1]
    whole = jnp.floor(count)
    rest = count - whole
    second = jnp.floor(rest * 256.0) * (1.0 / 256.0)
    rest = rest - second
    third = jnp.floor(rest * 65536.0) * (1.0 / 65536.0)
    row = lax.broadcasted_iota(jnp.int32, (8, 128), 0)
    parts = jnp.where(row == 0, whole, jnp.where(row == 1, second, jnp.where(row == 2, third, rest - third)))
    parts = jnp.where(row < 4, parts, 0.0)
    if width > 128:
        parts = jnp.concatenate([parts, jnp.zeros((8, width - 128), jnp.float32)], axis=1)
    return parts, jnp.zeros((rows - 8, width), jnp.float32)


def count_in(tail):
    return jnp.broadcast_to(jnp.sum(tail[:8, :128], axis=0, keepdims=True), LANES)


def outer_rows(at, rows, scale, operands):
    hidden_a, hidden_b, masked_a, masked_b = operands
    total = None
    for e in range(4):
        hidden, masked = ((hidden_a, masked_a), (hidden_b, masked_b))[e // 2]
        piece = scale[e, :1, :1] * dot(hidden[e % 2, at : at + rows, :], masked[e % 2], (1, 0))
        total = piece if total is None else total + piece
    return total


def outer_first_kernel(examples, *refs):
    small, operands, (out, count_out, scale_out) = refs[:5], refs[5:9], refs[9:]
    scale, count = factors_of(examples, *small)
    count_out[...] = count
    scale_out[...] = scale
    write_message(0, scale, count, operands, out)


def write_message(number, scale, count, operands, out):
    rows = out.shape[0] - TAIL
    total = outer_rows(number * rows, rows, scale, operands)
    out[...] = jnp.concatenate([total, *tail_rows(count, TAIL, out.shape[1])], axis=0).astype(out.dtype)


def outer_first(rows, examples, small, operands):
    outs = (
        array((rows + TAIL, operands[2].shape[2]), jnp.bfloat16),
        array(LANES, jnp.float32),
        array((4, *LANES), jnp.float32),
    )
    return call(lambda *refs: outer_first_kernel(examples, *refs), "outer_first", outs, (*small, *operands))


def outer_next(number, rows, scale, count, operands):
    out = array((rows + TAIL, operands[2].shape[2]), jnp.bfloat16)

    def kernel(scale, count, *refs):
        write_message(number, scale[...], count[...], refs[:4], refs[4])

    return call(kernel, "outer_next", out, (scale, count, *operands))


def outer_keep(rows, scale, operands):
    def kernel(scale, *refs):
        refs[4][...] = outer_rows(3 * rows, rows, scale[...], refs[:4])

    return call(kernel, "outer_keep", array((rows, operands[2].shape[2]), jnp.float32), (scale, *operands))


SIDE = 128


def step_join_kernel(count, kept, got0, got1, got2, send):
    rows = kept.shape[0]
    total, counted = kept[...], count[...]
    for got in (got0, got1, got2):
        message = got[...].astype(jnp.float32)
        total = total + message[:rows]
        counted = counted + count_in(message[rows:])
    side = jnp.concatenate(list(tail_rows(counted, 24, SIDE)) * (rows // 24), axis=0)
    send[...] = jnp.concatenate([total, side], axis=1).astype(send.dtype)


def step_join(count, kept, *got):
    rows, width = kept.shape
    return call(step_join_kernel, "step_join", array((rows, width + SIDE), jnp.bfloat16), (count, kept, *got))


def step_last_kernel(examples, ratio, noise, got, out, ratio_next):
    rows, width = out.shape
    message = got[...].astype(jnp.float32)
    chunks = [message[at : at + rows] for at in range(0, message.shape[0], rows)]
    while len(chunks) > 1:
        chunks = [a + b for a, b in zip(chunks[::2], chunks[1::2])]
    out[...] = chunks[0][:, :width]
    count = jnp.sum(chunks[0][:8, width:], axis=0, keepdims=True)
    share = (count[:, :1] + noise[...]) / examples
    ratio_next[...] = ratio[...] * jnp.exp(-(share - target_share))


def step_last(examples, ratio, noise, got, rows, width):
    outs = (array((rows, width), jnp.float32), array((1, 1), jnp.float32))
    args = (ratio.reshape(1, 1), noise.reshape(1, 1), got)
    return call(lambda *refs: step_last_kernel(examples, *refs), "step_last", outs, args)


def right(x, y, z, core):
    return (x + 1, y, z, core)


def left(x, y, z, core):
    return (x - 1, y, z, core)


def other_core(x, y, z, core):
    return (x, y, z, 1 - core)


def opposite(x, y, z, core):
    return (x + 2, y, z, core)


def swap_cores(*arrays):
    return [permute(array, other_core) for array in arrays]


def after(array, *others):
    return lax.optimization_barrier((array, *others))[0]


def per_device(inputs, cotangent, lengths, up_weight, down_weight, clip_ratio, count_noise):
    in_l = permute(inputs, right)
    masked = call(
        mask_kernel, "mask", array(cotangent.shape, cotangent.dtype), (lengths.reshape(1, -1), cotangent)
    )
    co_r = permute(masked, left)

    table = jnp.asarray(row_table())
    width, units = up_weight.shape
    up = select(up_kernel, "select_up", table, up_weight, (width, units // 2), units // 2)
    down = select(down_kernel, "select_down", table, down_weight, (units // 2, width), units // 2)

    in_s, co_s = swap_cores(inputs, masked)
    co_l = permute(masked, right)
    in_r = permute(inputs, left)
    early = early_pass((inputs, in_s), (masked, co_s), up, down)
    ratio = permute(after(clip_ratio.reshape(1, 1), up, down), other_core)
    in_l, in_r, co_l, co_r = (after(part, ratio) for part in (in_l, in_r, co_l, co_r))
    in_o = permute(in_l, right)
    co_o = permute(co_r, left)
    in_ls, in_rs, co_ls, co_rs = swap_cores(in_l, in_r, co_l, co_r)
    hidden_theirs, masked_theirs, squares_theirs = theirs_pass(
        (in_l, in_ls, in_r, in_rs), (co_l, co_ls, co_r, co_rs), *after((up, down), *early)
    )
    in_os, co_os = swap_cores(after(in_o, squares_theirs), after(co_o, squares_theirs))
    hidden_ours, masked_ours, squares = ours_pass(
        (inputs, in_s, in_o, in_os), (masked, co_s, co_o, co_os), up, down, early, squares_theirs
    )

    chip = call(add_kernel, "chip_squares", array(squares.shape, squares.dtype), (squares, permute(squares, other_core)))
    small = (ratio, chip, *(permute(chip, move) for move in (opposite, right, left)))
    examples_all = lax.axis_size("dp") * lengths.shape[0]
    operands = (hidden_ours, hidden_theirs, masked_ours, masked_theirs)
    quarter = units // 8
    send, count, scale = outer_first(quarter, examples_all, small, operands)
    got = [exchange(send, 0)]
    got += [exchange(outer_next(number, quarter, scale, count, operands), number) for number in (1, 2)]
    send = step_join(count, outer_keep(quarter, scale, operands), *got)
    got = lax.all_to_all(send, AXES, 0, 0, axis_index_groups=GROUPS, tiled=True)
    grad_down, ratio_next = step_last(
        examples_all, ratio, count_noise, got, 4 * quarter // (Z * Y), send.shape[1] - SIDE
    )
    return (grad_down, ratio_next.reshape(1))


def solution(mesh):
    return jax.shard_map(
        per_device,
        mesh=mesh,
        in_specs=(
            P("dp", "mp", None),
            P("dp", "mp", None),
            P("dp"),
            P(None, "mp"),
            P("mp", None),
            P(),
            P(),
        ),
        out_specs=(P(("mp", "dp"), None), P()),
        check_vma=False,
    )
```

```python
import jax
import jax.numpy as jnp
import numpy as np
from jax import lax
from jax.experimental import pallas as pl
from jax.experimental.pallas import tpu as pltpu
from jax.sharding import PartitionSpec as P

D = 1152
FF = 6144
SEQ = 256
AXES = ("dp", "mp")

curve_scale = 0.7978845608028654
cubic_term = 0.044715
target_share = 0.5

X, Y, Z, CORES = 4, 4, 8, 2


def coords(i):
    dp, mp = divmod(i, 4)
    z, rest = divmod(dp, 8)
    y, x_lo = divmod(rest, 2)
    x_hi, core = divmod(mp, 2)
    return (x_hi * 2 + x_lo, y, z, core)


def index_of(x, y, z, core):
    x, y, z = x % X, y % Y, z % Z
    return (z * 8 + y * 2 + x % 2) * 4 + (x // 2) * 2 + core


def permute(array, move):
    pairs = [(i, index_of(*move(*coords(i)))) for i in range(X * Y * Z * CORES)]
    return lax.ppermute(array, AXES, pairs)


def z_even(z, y):
    return (z ^ 1, y)


def z_odd(z, y):
    return ((((z - 1) % Z) ^ 1) + 1) % Z, y


def y_even(z, y):
    return (z, y ^ 1)


def y_odd(z, y):
    return (z, ((((y - 1) % Y) ^ 1) + 1) % Y)


STEPS = (
    ((z_even, z_odd), (z_odd, z_even)),
    ((y_even, y_odd), (y_odd, y_even)),
)


def group_of(core, z, y):
    if core == 0:
        return [(zb, yb) for zb in sorted((z, (z + 4) % Z)) for yb in range(Y)]
    return [(zb, y) for zb in range(Z)]


GROUPS = []
for _i in range(X * Y * Z * CORES):
    _x, _y, _z, _core = coords(_i)
    _group = [index_of(_x, yb, zb, _core) for zb, yb in group_of(_core, _z, _y)]
    if _group not in GROUPS:
        GROUPS.append(_group)


def row_table():
    table = np.zeros((CORES, Z, Y, 2, 2, 192), np.int32)
    for core in range(CORES):
        for chain in range(2):
            places = [(z, y) for z in range(Z) for y in range(Y)]
            orders = {place: group_of(core, *place) for place in places}
            for step in reversed(STEPS[core][chain]):
                orders = {place: orders[place] + orders[step(*place)] for place in places}
            for (z, y), order in orders.items():
                assert len(set(order)) == Z * Y
                rows = []
                for number, (zb, yb) in enumerate(order):
                    first = (16, 8)[number % 2]
                    cut = range(first) if chain == 0 else range(first, 24)
                    rows += [(zb * Y + yb) * 48 + row for row in cut]
                table[core, z, y, 0, chain] = rows[192:]
                table[core, z, y, 1, chain] = rows[:192]
    return table.reshape(CORES * Z * Y, 1, -1)


def exchange(array, number, chain):
    def move(x, y, z, core):
        z, y = STEPS[core][chain][number](z, y)
        return (x, y, z, core)

    return permute(array, move)


def gelu_parts(preact):
    square = preact * preact
    half = 0.5 * jnp.tanh(preact * (curve_scale + (curve_scale * cubic_term) * square)) + 0.5
    values = preact * half
    slopes = half + values * (1.0 - half) * (2.0 * curve_scale + (6.0 * curve_scale * cubic_term) * square)
    return (values, slopes)


def dot(left, right, contract):
    return lax.dot_general(left, right, ((contract[:1], contract[1:]), ((), ())), preferred_element_type=jnp.float32)


VMEM = pl.BlockSpec(memory_space=pltpu.VMEM)
HBM = pl.BlockSpec(memory_space=pl.ANY)
LANES = (8, 128)


def call(kernel, name, outs, args, specs=None, scratch=(), flops=0, limit=12):
    return pl.pallas_call(
        kernel,
        out_shape=outs,
        in_specs=specs or [VMEM] * len(args),
        out_specs=jax.tree.map(lambda _: VMEM, outs),
        scratch_shapes=scratch,
        compiler_params=pltpu.CompilerParams(vmem_limit_bytes=limit * 2**20),
        cost_estimate=pl.CostEstimate(flops=flops, bytes_accessed=0, transcendentals=0),
        name=name,
    )(*args)


def array(shape, kind):
    return jax.ShapeDtypeStruct(shape, kind)


def place():
    dp, mp = lax.axis_index("dp"), lax.axis_index("mp")
    return dp // 8, (dp // 2) % 4, dp % 2, mp % 2


def mask_kernel(lengths, cotangent, out):
    positions = lax.axis_index("mp") * out.shape[1] + lax.broadcasted_iota(jnp.int32, out.shape[1:], 0)
    for e in range(out.shape[0]):
        value = cotangent[e].astype(jnp.float32)
        out[e] = jnp.where(positions < lengths[:, e : e + 1], value, 0.0).astype(out.dtype)


def load_rows(table, rows, sem):
    z, y, x_lo, core = place()
    copy = pltpu.make_async_copy(table.at[(core * Z + z) * Y + y], rows, sem)
    copy.start()
    copy.wait()
    return rows[...] + x_lo * 24


def up_kernel(table, weight, out, rows, sem):
    chosen = load_rows(table, rows, sem)
    pick = lax.broadcasted_iota(jnp.int32, (weight.shape[1], out.shape[1]), 0) == chosen
    out[...] = dot(weight[...], pick.astype(jnp.bfloat16), (1, 0)).astype(out.dtype)


def down_kernel(table, weight, out, rows, sem):
    chosen = load_rows(table, rows, sem).astype(jnp.float32)
    chosen = jnp.broadcast_to(chosen, (8, chosen.shape[1])).T[:, :1].astype(jnp.int32)
    pick = lax.broadcasted_iota(jnp.int32, (out.shape[0], weight.shape[0]), 1) == chosen
    out[...] = dot(pick.astype(jnp.bfloat16), weight[...], (1, 0)).astype(out.dtype)


def select(kernel, name, table, weight, shape, units):
    scratch = [pltpu.VMEM(table.shape[1:], jnp.int32), pltpu.SemaphoreType.DMA]
    return call(kernel, name, array(shape, weight.dtype), (table, weight), [HBM, VMEM], scratch, limit=16)


def products_of(rows, masked, up, down):
    values, slopes = gelu_parts(dot(rows, up[...], (1, 0)))
    delta = dot(masked, down[...], (1, 1)) * slopes
    return values.astype(jnp.bfloat16), delta.astype(jnp.bfloat16)


def stacked(refs, e):
    return jnp.concatenate([ref[e] for ref in refs], axis=0)


def both_examples(refs):
    return jnp.concatenate([stacked(refs, e) for e in range(2)], axis=0)


def square_of(rows, masked, hidden, delta):
    first = dot(rows, rows, (1, 1)) * dot(delta, delta, (1, 1))
    second = dot(hidden, hidden, (1, 1)) * dot(masked, masked, (1, 1))
    return jnp.broadcast_to(jnp.sum(first + second), LANES)


def early_kernel(in_a, in_b, co_a, co_b, up, down, hidden, delta):
    hidden[...], delta[...] = products_of(both_examples((in_a, in_b)), both_examples((co_a, co_b)), up, down)


def early_pass(inputs, cotans, up, down):
    out = array((4 * inputs[0].shape[1], up.shape[1]), jnp.bfloat16)
    return call(early_kernel, "early_pass", (out, out), (*inputs, *cotans, up, down))


def theirs_kernel(*refs):
    inputs, cotans = refs[:4], refs[4:8]
    up, down, hidden_out, masked_out, squares_out = refs[8:]
    for e in range(2):
        rows, masked = stacked(inputs, e), stacked(cotans, e)
        hidden, delta = products_of(rows, masked, up, down)
        hidden_out[e] = hidden.T
        masked_out[e] = masked
        squares_out[e] = square_of(rows, masked, hidden, delta)


def pass_outs(units, tokens, width, squares):
    return (
        array((2, units, tokens), jnp.bfloat16),
        array((2, tokens, width), jnp.bfloat16),
        array((squares, *LANES), jnp.float32),
    )


def theirs_pass(inputs, cotans, up, down):
    width, units = up.shape
    tokens = 4 * inputs[0].shape[1]
    return call(theirs_kernel, "theirs_pass", pass_outs(units, tokens, width, 2), (*inputs, *cotans, up, down))


def ours_kernel(*refs):
    inputs, cotans = refs[:4], refs[4:8]
    up, down, hidden_early, delta_early, theirs = refs[8:13]
    hidden_out, masked_out, squares_out = refs[13:]
    hidden_late, delta_late = products_of(both_examples(inputs[2:]), both_examples(cotans[2:]), up, down)
    half = hidden_late.shape[0] // 2
    is_first = place()[2] == 0
    for e in range(2):
        at = slice(e * half, (e + 1) * half)
        rows, masked = stacked(inputs, e), stacked(cotans, e)
        hidden = jnp.concatenate([hidden_early[at, :], hidden_late[at, :]], axis=0)
        delta = jnp.concatenate([delta_early[at, :], delta_late[at, :]], axis=0)
        hidden_out[e] = hidden.T
        masked_out[e] = masked
        square = square_of(rows, masked, hidden, delta)
        squares_out[e] = jnp.where(is_first, square, theirs[e])
        squares_out[2 + e] = jnp.where(is_first, theirs[e], square)


def ours_pass(inputs, cotans, up, down, early, theirs):
    width, units = up.shape
    tokens = 4 * inputs[0].shape[1]
    outs = pass_outs(units, tokens, width, 4)
    return call(ours_kernel, "ours_pass", outs, (*inputs, *cotans, up, down, *early, theirs))


def add_kernel(left, right, out):
    out[...] = left[...] + right[...]


def factors_of(examples, ratio, chip, across, from_left, from_right):
    total = (chip[...] + across[...]) + (from_left[...] + from_right[...])
    norms = jnp.sqrt(total)
    clip = ratio[...] * np.sqrt(np.float32(SEQ * D * FF))
    factors = clip / jnp.maximum(norms, clip)
    is_first = place()[2] == 0
    scale = jnp.where(is_first, factors, jnp.concatenate([factors[2:], factors[:2]], axis=0)) * (1.0 / examples)
    soft = jnp.floor(jax.nn.sigmoid(4.0 * (clip - norms) / clip) * 131072.0 + 0.5) * (1.0 / 131072.0)
    return scale, (soft[0] + soft[1]) + (soft[2] + soft[3])


TAIL = 16


def tail_rows(count, rows, width):
    count = count[:1, :1]
    whole = jnp.floor(count)
    rest = count - whole
    second = jnp.floor(rest * 256.0) * (1.0 / 256.0)
    rest = rest - second
    third = jnp.floor(rest * 65536.0) * (1.0 / 65536.0)
    row = lax.broadcasted_iota(jnp.int32, (8, 128), 0)
    parts = jnp.where(row == 0, whole, jnp.where(row == 1, second, jnp.where(row == 2, third, rest - third)))
    parts = jnp.where(row < 4, parts, 0.0)
    if width > 128:
        parts = jnp.concatenate([parts, jnp.zeros((8, width - 128), jnp.float32)], axis=1)
    return parts, jnp.zeros((rows - 8, width), jnp.float32)


def count_in(tail):
    return jnp.broadcast_to(jnp.sum(tail[:8, :128], axis=0, keepdims=True), LANES)


def outer_rows(at, rows, scale, operands):
    hidden_a, hidden_b, masked_a, masked_b = operands
    total = None
    for e in range(4):
        hidden, masked = ((hidden_a, masked_a), (hidden_b, masked_b))[e // 2]
        piece = scale[e, :1, :1] * dot(hidden[e % 2, at : at + rows, :], masked[e % 2], (1, 0))
        total = piece if total is None else total + piece
    return total


def outer_first_kernel(examples, *refs):
    small, operands, (out, count_out, scale_out) = refs[:5], refs[5:9], refs[9:]
    rows, width = out.shape[0] - TAIL, out.shape[1]
    scale, count = factors_of(examples, *small)
    count_out[...] = count
    scale_out[...] = scale
    total = outer_rows(0, rows, scale, operands)
    out[...] = jnp.concatenate([total, *tail_rows(count, TAIL, width)], axis=0).astype(out.dtype)


def outer_second_kernel(scale, *refs):
    operands, out = refs[:4], refs[4]
    rows = out.shape[0]
    out[...] = outer_rows(rows, rows, scale[...], operands).astype(out.dtype)


def outer_keep_kernel(scale, *refs):
    operands, outs = refs[:4], refs[4:]
    rows = outs[0].shape[0]
    for chain, out in enumerate(outs):
        out[...] = outer_rows((2 + chain) * rows, rows, scale[...], operands)


def outer_first(rows, examples, small, operands):
    outs = (
        array((rows + TAIL, operands[2].shape[2]), jnp.bfloat16),
        array(LANES, jnp.float32),
        array((4, *LANES), jnp.float32),
    )
    return call(lambda *refs: outer_first_kernel(examples, *refs), "outer_first", outs, (*small, *operands))


def outer_second(rows, scale, operands):
    out = array((rows, operands[2].shape[2]), jnp.bfloat16)
    return call(outer_second_kernel, "outer_second", out, (scale, *operands))


def outer_keep(rows, scale, operands):
    outs = (array((rows, operands[2].shape[2]), jnp.float32),) * 2
    return call(outer_keep_kernel, "outer_keep", outs, (scale, *operands))


def step_first_kernel(count, kept, got, count_out, keep, send):
    rows, width = kept.shape
    half = rows // 2
    message = got[...].astype(jnp.float32)
    total = kept[...] + message[:rows]
    keep[...] = total[:half]
    counted = count[...] + count_in(message[rows:])
    count_out[...] = counted
    send[...] = jnp.concatenate([total[half:], *tail_rows(counted, TAIL, width)], axis=0).astype(send.dtype)


def step_outs(kept, sent, width):
    return (array(LANES, jnp.float32), array((kept, width), jnp.float32), array((sent, width), jnp.bfloat16))


def step_first(count, kept, got):
    rows, width = kept.shape
    return call(step_first_kernel, "step_first", step_outs(rows // 2, rows // 2 + TAIL, width), (count, kept, got))


def step_second_kernel(kept, got, keep, send):
    half = kept.shape[0] // 2
    total = kept[...] + got[...].astype(jnp.float32)
    keep[...] = total[:half]
    send[...] = total[half:].astype(send.dtype)


def step_second(kept, got):
    rows, width = kept.shape
    outs = (array((rows // 2, width), jnp.float32), array((rows // 2, width), jnp.bfloat16))
    return call(step_second_kernel, "step_second", outs, (kept, got))


SIDE = 128


def step_join_kernel(count, kept0, kept1, got0, got1, send):
    rows, width = kept0.shape
    message = got0[...].astype(jnp.float32)
    total0 = kept0[...] + message[:rows]
    total1 = kept1[...] + got1[...].astype(jnp.float32)
    counted = count[...] + count_in(message[rows:])
    pieces = []
    for at in range(0, rows, 24):
        pieces += [total0[at : at + 16], total1[at : at + 8], total0[at + 16 : at + 24], total1[at + 8 : at + 24]]
    side = tail_rows(counted, 24, SIDE)
    side = jnp.concatenate(list(side) * (rows // 12), axis=0)
    send[...] = jnp.concatenate([jnp.concatenate(pieces, axis=0), side], axis=1).astype(send.dtype)


def step_join(count, kept0, kept1, got0, got1):
    rows, width = kept0.shape
    return call(step_join_kernel, "step_join", array((2 * rows, width + SIDE), jnp.bfloat16), (count, kept0, kept1, got0, got1))


def step_last_kernel(examples, ratio, noise, got, out, ratio_next):
    rows, width = out.shape
    message = got[...].astype(jnp.float32)
    chunks = [message[at : at + rows] for at in range(0, message.shape[0], rows)]
    while len(chunks) > 1:
        chunks = [a + b for a, b in zip(chunks[::2], chunks[1::2])]
    out[...] = chunks[0][:, :width]
    count = jnp.sum(chunks[0][:8, width:], axis=0, keepdims=True)
    share = (count[:, :1] + noise[...]) / examples
    ratio_next[...] = ratio[...] * jnp.exp(-(share - target_share))


def step_last(examples, ratio, noise, got, rows, width):
    outs = (array((rows, width), jnp.float32), array((1, 1), jnp.float32))
    args = (ratio.reshape(1, 1), noise.reshape(1, 1), got)
    return call(lambda *refs: step_last_kernel(examples, *refs), "step_last", outs, args)


def right(x, y, z, core):
    return (x + 1, y, z, core)


def left(x, y, z, core):
    return (x - 1, y, z, core)


def other_core(x, y, z, core):
    return (x, y, z, 1 - core)


def opposite(x, y, z, core):
    return (x + 2, y, z, core)


def swap_cores(*arrays):
    return [permute(array, other_core) for array in arrays]


def after(array, *others):
    return lax.optimization_barrier((array, *others))[0]


def per_device(inputs, cotangent, lengths, up_weight, down_weight, clip_ratio, count_noise):
    in_l = permute(inputs, right)
    masked = call(
        mask_kernel, "mask", array(cotangent.shape, cotangent.dtype), (lengths.reshape(1, -1), cotangent)
    )
    co_r = permute(masked, left)

    table = jnp.asarray(row_table())
    width, units = up_weight.shape
    up = select(up_kernel, "select_up", table, up_weight, (width, units // 2), units // 2)
    down = select(down_kernel, "select_down", table, down_weight, (units // 2, width), units // 2)

    in_s, co_s = swap_cores(inputs, masked)
    co_l = permute(masked, right)
    in_r = permute(inputs, left)
    early = early_pass((inputs, in_s), (masked, co_s), up, down)
    ratio = permute(after(clip_ratio.reshape(1, 1), up, down), other_core)
    in_l, in_r, co_l, co_r = (after(part, ratio) for part in (in_l, in_r, co_l, co_r))
    in_o = permute(in_l, right)
    co_o = permute(co_r, left)
    in_ls, in_rs, co_ls, co_rs = swap_cores(in_l, in_r, co_l, co_r)
    hidden_theirs, masked_theirs, squares_theirs = theirs_pass(
        (in_l, in_ls, in_r, in_rs), (co_l, co_ls, co_r, co_rs), *after((up, down), *early)
    )
    in_os, co_os = swap_cores(after(in_o, squares_theirs), after(co_o, squares_theirs))
    hidden_ours, masked_ours, squares = ours_pass(
        (inputs, in_s, in_o, in_os), (masked, co_s, co_o, co_os), up, down, early, squares_theirs
    )

    chip = call(add_kernel, "chip_squares", array(squares.shape, squares.dtype), (squares, permute(squares, other_core)))
    small = (ratio, chip, *(permute(chip, move) for move in (opposite, right, left)))
    examples_all = lax.axis_size("dp") * lengths.shape[0]
    operands = (hidden_ours, hidden_theirs, masked_ours, masked_theirs)
    quarter = units // 8
    send0, count, scale = outer_first(quarter, examples_all, small, operands)
    send1 = outer_second(quarter, scale, operands)
    got0, got1 = exchange(send0, 0, 0), exchange(send1, 0, 1)
    keep0, keep1 = outer_keep(quarter, scale, operands)
    count, keep0, send0 = step_first(count, keep0, got0)
    got0 = exchange(send0, 1, 0)
    keep1, send1 = step_second(keep1, got1)
    got1 = exchange(send1, 1, 1)
    send = step_join(count, keep0, keep1, got0, got1)
    got = lax.all_to_all(send, AXES, 0, 0, axis_index_groups=GROUPS, tiled=True)
    grad_down, ratio_next = step_last(
        examples_all, ratio, count_noise, got, 4 * quarter // (Z * Y), send.shape[1] - SIDE
    )
    return (grad_down, ratio_next.reshape(1))


def solution(mesh):
    return jax.shard_map(
        per_device,
        mesh=mesh,
        in_specs=(
            P("dp", "mp", None),
            P("dp", "mp", None),
            P("dp"),
            P(None, "mp"),
            P("mp", None),
            P(),
            P(),
        ),
        out_specs=(P(("mp", "dp"), None), P()),
        check_vma=False,
    )
```
